32 devices in a mesh: expert: 16 (over z, y, core), dp: 2 (over x).
Axes of the slice: x: 2, y: 2, z: 4, core: 2. Of those that a mesh axis runs over, the one named last changes fastest.
Arguments:
- tokens_in: bfloat16 [8192, 1024], P(('expert', 'dp')), may hold values from -6 to 6
- out_grad: bfloat16 [8192, 1024], P(('expert', 'dp')), may hold values from -4 to 4
- gates: bfloat16 [8192], P(('expert', 'dp')), may hold values from 0.19921875 to 1
- expert_ids: int32 [8192], P(('expert', 'dp')), may hold values from 0 to 7, as said below
- slot_ids: int32 [8192], P(('expert', 'dp')), may hold values from 0 to 35
- w_up: bfloat16 [16, 1024, 1024], P('expert'), may hold values from -0.1875 to 0.1875
- w_down: bfloat16 [16, 1024, 1024], P('expert'), may hold values from -0.125 to 0.125
Outputs:
- in_grad: bfloat16 [8192, 1024], P(('expert', 'dp'))
- gate_grad: bfloat16 [8192], P(('expert', 'dp'))
- up_grad: bfloat16 [16, 1024, 1024], P('expert', 'dp')
- down_grad: bfloat16 [16, 1024, 1024], P('expert', 'dp')
The draws below stay inside these ranges and needn't reach their ends.
Inputs may be any that keep to these rules, and one draw needn't show every extreme that they name: `expert_ids`: the tokens of one device (aligned blocks of 256) take distinct pairs of expert and slot; no expert receives more than 36 tokens of one device, and one expert receives exactly 36 from every device.
All inputs are finite; a program needn't handle non-finite values.
Results may differ from the reference program's by a relative error of at most 0.015.
Values may be sent and summed in bfloat16 or wider, within the bound.
A program may use at most 64 MiB of HBM per device.

```python
import jax
import jax.numpy as jnp
from jax import lax

D = 1024
H = 2048
TOK_DEV = 256
H_DEV = 1024
EXPERTS = 8
PIECES = 16
CAP = 36
REPLICAS = 2
TOKENS = 8192
EXP_ROWS = 1152
N_EXPERT = 16


def routing_pairs(key):
    base = jax.random.fold_in(key, 4177)
    key_load, key_full, key_noise, key_order = jax.random.split(base, 4)
    blocks = TOKENS // TOK_DEV
    cells = EXPERTS * CAP
    level = jax.random.randint(key_load, (EXPERTS,), 0, 4)
    full_one = jax.random.randint(key_full, (), 0, EXPERTS)
    level = jnp.where(jnp.arange(EXPERTS, dtype=jnp.int32) == full_one, 64, level)
    noise = jax.random.randint(key_noise, (blocks, cells), 0, 16384)
    cell_ids = jnp.arange(cells, dtype=jnp.int32)
    score = (jnp.repeat(level, CAP)[None, :] * 4096 + noise) * cells + cell_ids[None, :]
    chosen = lax.top_k(score, TOK_DEV)[1].astype(jnp.int32)
    order_keys = jax.random.split(key_order, blocks)
    orders = jax.vmap(lambda k: jax.random.permutation(k, TOK_DEV))(order_keys)
    chosen = jnp.take_along_axis(chosen, orders.astype(jnp.int32), axis=1)
    experts_of = (chosen // CAP).reshape(TOKENS).astype(jnp.int32)
    slots_of = (chosen % CAP).reshape(TOKENS).astype(jnp.int32)
    return (experts_of, slots_of)


def draw_expert_ids(key, part):
    return routing_pairs(key)[0]


def draw_slot_ids(key, part):
    return routing_pairs(key)[1]


def shard_levels(key, extent, pieces, least, top_value):
    level, own = 1.0, jax.random.fold_in(key, 6)
    for position, blocks in pieces:
        steps = jnp.exp(jax.random.uniform(jax.random.fold_in(own, position), (blocks,), jnp.float32, least / len(pieces), top_value / len(pieces)))
        level = level * jnp.repeat(steps, extent[position] // blocks).reshape([-1 if axis == position else 1 for axis in range(len(extent))])
    return level


def scatter_about(key, extent, width, bound, cuts=(), kind=jnp.bfloat16):
    loudness = shard_levels(key, extent, cuts, -0.22, 0.18) if cuts else 1.0
    drawn = jax.random.normal(key, extent, jnp.float32) * width * loudness
    return jnp.minimum(jnp.maximum(drawn, -bound), bound).astype(kind)


def setup_inputs(seed: int = 0) -> dict:
    seeds = jax.random.split(jax.random.key(seed), 8)
    tokens_in = scatter_about(seeds[0], (TOKENS, D), 1.0, 6.0, ((0, 32),))
    out_grad = scatter_about(seeds[1], (TOKENS, D), 0.5, 4.0, ((0, 32),))
    gates = jnp.clip(0.19921875 + 0.80078125 * jax.random.uniform(seeds[2], (TOKENS,), jnp.float32) ** shard_levels(seeds[2], (TOKENS,), ((0, 32),), -0.2, 0.2), 0.19921875, 1.0).astype(jnp.bfloat16)
    expert_ids = draw_expert_ids(jax.random.fold_in(seeds[7], 71), 0)
    slot_ids = draw_slot_ids(jax.random.fold_in(seeds[7], 71), 0)
    w_up = scatter_about(seeds[5], (PIECES, D, H_DEV), D ** -0.5, 0.1875, ((0, 16),))
    w_down = scatter_about(seeds[6], (PIECES, H_DEV, D), H ** -0.5, 0.125, ((0, 16),))
    return dict(tokens_in=tokens_in, out_grad=out_grad, gates=gates, expert_ids=expert_ids, slot_ids=slot_ids, w_up=w_up, w_down=w_down)


def gelu_parts(hidden):
    cdf = 0.5 * (1.0 + lax.erf(hidden * 0.7071067811865476))
    pdf = jnp.exp(-0.5 * hidden * hidden) * 0.3989422804014327
    return hidden * cdf, cdf + hidden * pdf


def group_sum(left, right):
    width_left = left.shape[1]
    width_right = right.shape[1]
    left_g = left.reshape(N_EXPERT, REPLICAS, CAP, width_left).transpose(1, 0, 2, 3).reshape(REPLICAS, N_EXPERT * CAP, width_left)
    right_g = right.reshape(N_EXPERT, REPLICAS, CAP, width_right).transpose(1, 0, 2, 3).reshape(REPLICAS, N_EXPERT * CAP, width_right)
    parts = []
    for group in range(REPLICAS):
        parts.append(jnp.dot(left_g[group].T, right_g[group], preferred_element_type=jnp.float32).astype(jnp.bfloat16))
    stacked = lax.optimization_barrier(jnp.stack(parts))
    return jnp.sum(stacked.astype(jnp.float32), axis=0).astype(jnp.bfloat16)


def reference(tokens_in, out_grad, gates, expert_ids, slot_ids, w_up, w_down):
    owner = (jnp.arange(TOKENS, dtype=jnp.int32) // TOK_DEV).astype(jnp.int32)
    place = (expert_ids * EXP_ROWS + owner * CAP + slot_ids).astype(jnp.int32)
    x_slots = jnp.zeros((EXPERTS * EXP_ROWS, D), jnp.bfloat16).at[place].set(tokens_in).reshape(EXPERTS, EXP_ROWS, D)
    g_slots = jnp.zeros((EXPERTS * EXP_ROWS, D), jnp.bfloat16).at[place].set(out_grad).reshape(EXPERTS, EXP_ROWS, D)
    gate_slots = jnp.zeros((EXPERTS * EXP_ROWS,), jnp.bfloat16).at[place].set(gates).reshape(EXPERTS, EXP_ROWS)
    up_pairs = w_up.reshape(EXPERTS, 2, D, H_DEV)
    down_pairs = w_down.reshape(EXPERTS, 2, H_DEV, D)

    def one_expert(items):
        x_rows, g_rows, gate_rows, up_pair, down_pair = items
        d_in = (gate_rows.astype(jnp.float32)[:, None] * g_rows.astype(jnp.float32)).astype(jnp.bfloat16)
        d_total = jnp.zeros((EXP_ROWS, D), jnp.float32)
        gate_total = jnp.zeros((EXP_ROWS,), jnp.float32)
        ups = []
        downs = []
        for half in range(2):
            hidden = jnp.dot(x_rows, up_pair[half], preferred_element_type=jnp.float32)
            value, slope = gelu_parts(hidden)
            act = value.astype(jnp.bfloat16)
            out_part = lax.optimization_barrier(jnp.dot(act, down_pair[half], preferred_element_type=jnp.float32).astype(jnp.bfloat16))
            gate_part = lax.optimization_barrier(jnp.sum(g_rows.astype(jnp.float32) * out_part.astype(jnp.float32), axis=-1).astype(jnp.bfloat16))
            d_act = jnp.dot(d_in, down_pair[half].T, preferred_element_type=jnp.float32)
            d_hidden = (d_act * slope).astype(jnp.bfloat16)
            d_part = lax.optimization_barrier(jnp.dot(d_hidden, up_pair[half].T, preferred_element_type=jnp.float32).astype(jnp.bfloat16))
            d_total = d_total + d_part.astype(jnp.float32)
            gate_total = gate_total + gate_part.astype(jnp.float32)
            ups.append(group_sum(x_rows, d_hidden))
            downs.append(group_sum(act, d_in))
        return d_total.astype(jnp.bfloat16), gate_total.astype(jnp.bfloat16), jnp.stack(ups), jnp.stack(downs)

    d_rows, gate_rows, up_grad, down_grad = lax.map(one_expert, (x_slots, g_slots, gate_slots, up_pairs, down_pairs))
    in_grad = d_rows.reshape(EXPERTS * EXP_ROWS, D)[place]
    gate_grad = gate_rows.reshape(EXPERTS * EXP_ROWS)[place]
    return in_grad, gate_grad, up_grad.reshape(PIECES, D, H_DEV), down_grad.reshape(PIECES, H_DEV, D)
```

```python
import functools

import jax
import jax.numpy as jnp
from jax import lax
from jax.experimental import pallas as pl
from jax.experimental.pallas import tpu as pltpu
from jax.sharding import PartitionSpec as P

F32 = jnp.float32
BF16 = jnp.bfloat16


def xor(a, b, count):
    total, bit = 0, 1
    while bit < count:
        total = total + lax.rem(a // bit + b // bit, 2) * bit
        bit *= 2
    return total


def gelu_parts(hidden):
    cdf = 0.5 * (1.0 + lax.erf(hidden * 0.7071067811865476))
    pdf = jnp.exp(-0.5 * hidden * hidden) * 0.3989422804014327
    return (hidden * cdf, cdf + hidden * pdf)


def dot(a, b, da, db):
    return lax.dot_general(a, b, (((da,), (db,)), ((), ())), preferred_element_type=F32)


def kernel(
    chips, dps, cap, rows,
    place_ref, gates_ref, tok_ref, cot_ref, up_hbm, down_hbm,
    in_ref, gate_ref, upg_ref, downg_ref,
    tx, rx, xc, dc, actc, dhc, part, sib, xr, fin, wu, wd, ugs, ugr,
    w_sem, ici_s, ici_r, sf_s, sf_r, xf_s, xf_r, ps_s, ps_r, xr_s, xr_r, fin_s, fin_r, ug_s, ug_r,
):
    me = lax.axis_index("expert")
    k = lax.axis_index("dp")
    g = me // 2
    c = lax.rem(me, 2)
    o = 1 - c
    width = tok_ref.shape[1]
    half = width // 2
    hq = wu.shape[1]
    dblk = width // dps
    per = 2 * dps * rows

    def dev(chip, core, dp):
        return {"expert": chip * 2 + core, "dp": dp}

    def other(j):
        return lax.rem(k + j, dps)

    def remote(src, dst, s, r, target):
        return pltpu.make_async_remote_copy(
            src_ref=src, dst_ref=dst, send_sem=s, recv_sem=r,
            device_id=target, device_id_type=pl.DeviceIdType.MESH,
        )

    def ici(i):
        return remote(tx.at[i], rx.at[i, c, k], ici_s.at[i], ici_r.at[i], dev(xor(g, i, chips), c, k))

    def side(i, core, kk):
        return remote(
            rx.at[i, core, kk], rx.at[i, core, kk], sf_s.at[i, kk], sf_r.at[i, kk], dev(g, o, k)
        )

    def cross(i, kk, slot):
        return remote(
            rx.at[i, c, slot], rx.at[i, c, slot], xf_s.at[i, kk], xf_r.at[i, slot], dev(g, c, kk)
        )

    def half_sum(i, kk):
        return remote(part.at[i, o, kk], sib.at[i, kk], ps_s.at[i, kk], ps_r.at[i, kk], dev(g, o, k))

    def cross_sum(i, kk, slot):
        return remote(
            part.at[i, c, kk], xr.at[i, slot], xr_s.at[i, kk], xr_r.at[i, slot], dev(g, c, kk)
        )

    def home(i):
        return remote(part.at[i, c, k], fin.at[i], fin_s.at[i], fin_r.at[i], dev(xor(g, i, chips), c, k))

    tile = min(256, dblk)
    tiles = dblk // tile

    def up_send(j, m, kk, slot):
        return remote(
            ugs.at[j - 1, pl.ds(m * tile, tile)], ugr.at[slot, pl.ds(m * tile, tile)],
            ug_s.at[kk, m], ug_r.at[slot, m], dev(g, c, kk),
        )

    load_up = pltpu.make_async_copy(
        up_hbm.at[0, :, pl.ds(pl.multiple_of(k * hq, hq), hq)], wu, w_sem.at[0]
    )
    load_down = pltpu.make_async_copy(
        down_hbm.at[0, pl.ds(pl.multiple_of(k * hq, hq), hq), :], wd, w_sem.at[1]
    )
    load_up.start()
    load_down.start()

    barrier = pltpu.get_barrier_semaphore()

    def greet(target):
        pl.semaphore_signal(barrier, inc=1, device_id=target, device_id_type=pl.DeviceIdType.MESH)

    @pl.loop(1, chips)
    def _(i):
        greet(dev(xor(g, i, chips), c, k))

    greet(dev(g, o, k))
    for j in range(1, dps):
        greet(dev(g, c, other(j)))

    eye = lax.broadcasted_iota(jnp.int32, (1, rows, 128), 1) == lax.broadcasted_iota(
        jnp.int32, (1, rows, 128), 2
    )
    at_cap = lax.broadcasted_iota(jnp.int32, (1, rows, 128), 1) == cap

    def one_hot():
        slots = lax.broadcasted_iota(jnp.int32, (chips * rows, tok_ref.shape[0]), 0)
        return slots == place_ref[...]

    hot = one_hot()
    hot16 = jnp.where(hot, 1.0, 0.0).astype(BF16)
    gate_col = jnp.sum(jnp.where(hot, gates_ref[...].astype(F32), 0.0), axis=1, keepdims=True)
    gate_row = jnp.sum(jnp.where(eye, gate_col.reshape(chips, rows, 1), 0.0), axis=1, keepdims=True)
    x_pack = dot(hot16, tok_ref[...], 1, 0).reshape(chips, rows, width)
    g_pack = dot(hot16, cot_ref[...], 1, 0).reshape(chips, rows, width)
    first = jnp.where(at_cap, gate_row, x_pack[:, :, :128])
    x_pack = jnp.concatenate([first, x_pack[:, :, 128:]], axis=2)
    both = jnp.concatenate([x_pack, g_pack], axis=1).astype(BF16)
    tx[...] = both
    rx[0, c, k] = both[0]

    pl.semaphore_wait(barrier, chips - 1 + 1 + dps - 1)

    @pl.loop(1, chips)
    def _(i):
        ici(i).start()

    def stage_a(i):
        @pl.when(i > 0)
        def _():
            ici(i).wait_recv()

        for j in range(1, dps):
            cross(i, other(j), k).start()
        side(i, c, k).start()

    def stage_b(i):
        for j in range(1, dps):
            cross(i, other(j), other(j)).wait_recv()
            side(i, c, other(j)).start()

    def stage_c(i):
        for kk in range(dps):
            side(i, o, kk).wait_recv()
        blk = rx[i].reshape(2 * dps, 2 * rows, width).astype(F32)
        x = blk[:, :rows].reshape(per, width).astype(BF16)
        cot = blk[:, rows:].reshape(per, width)
        gate = jnp.sum(
            jnp.where(eye, blk[:, cap : cap + 1, :128], 0.0), axis=2, keepdims=True
        ).reshape(per, 1)
        at = pl.ds(pl.multiple_of(i * per, per), per)
        xc[at, :] = x
        dc[at, :] = (gate * cot).astype(BF16)
        hidden = dot(x, wu[...], 1, 0)
        gv = dot(cot.astype(BF16), wd[...], 1, 1)
        value, slope = gelu_parts(hidden)
        act = value.astype(BF16)
        dh = (gate * gv * slope).astype(BF16)
        actc[at, :] = act
        dhc[at, :] = dh
        gp = jnp.sum(act.astype(F32) * gv, axis=1, keepdims=True).reshape(2 * dps, rows, 1)
        gp_row = jnp.sum(jnp.where(eye, gp, 0.0), axis=1, keepdims=True)
        d = dot(dh, wu[...], 1, 1).reshape(2 * dps, rows, width)
        lead = jnp.where(at_cap, gp_row, d[:, :, :128])
        left = jnp.concatenate([lead, d[:, :, 128:half]], axis=2)
        whole = jnp.concatenate([left, d[:, :, half:]], axis=1).astype(BF16)
        part[i] = whole.reshape(2, dps, 2 * rows, half)
        for kk in range(dps):
            half_sum(i, kk).start()

    def stage_d(i):
        for j in list(range(1, dps)) + [0]:
            kk = other(j)
            half_sum(i, kk).wait_recv()
            part[i, c, kk] = (part[i, c, kk].astype(F32) + sib[i, kk].astype(F32)).astype(BF16)
            if j:
                cross_sum(i, kk, dps - 1 - j).start()

    def stage_e(i):
        total = part[i, c, k].astype(F32)
        for j in range(1, dps):
            cross_sum(i, other(j), j - 1).wait_recv()
            total = total + xr[i, j - 1].astype(F32)
        total = total.astype(BF16)

        @pl.when(i > 0)
        def _():
            part[i, c, k] = total
            home(i).start()

        @pl.when(i == 0)
        def _():
            fin[0] = total

    load_up.wait()
    load_down.wait()

    @pl.loop(0, chips + 2)
    def _(t):
        @pl.when(t < chips)
        def _():
            stage_a(t)

        @pl.when(jnp.logical_and(t >= 1, t < chips + 1))
        def _():
            stage_b(t - 1)

        @pl.when(t >= 2)
        def _():
            stage_c(t - 2)

        @pl.when(t >= 3)
        def _():
            stage_d(t - 3)

        @pl.when(t >= 4)
        def _():
            stage_e(t - 4)

    stage_d(chips - 1)

    def up_tile(kk, m):
        at = pl.ds(pl.multiple_of(kk * dblk + m * tile, tile), tile)
        return dot(xc[:, at], dhc[...], 0, 0).astype(BF16)

    for j in range(1, dps):
        @pl.loop(0, tiles)
        def _(m):
            ugs[j - 1, pl.ds(pl.multiple_of(m * tile, tile), tile), :] = up_tile(other(j), m)
            up_send(j, m, other(j), dps - 1 - j).start()

    stage_e(chips - 2)
    stage_e(chips - 1)
    mine = pl.ds(pl.multiple_of(k * hq, hq), hq)

    @pl.loop(0, tiles)
    def _(m):
        upg_ref[pl.ds(pl.multiple_of(m * tile, tile), tile), mine] = up_tile(k, m)

    dtile = min(256, hq)

    @pl.loop(0, hq // dtile)
    def _(m):
        at = pl.ds(pl.multiple_of(m * dtile, dtile), dtile)
        downg_ref[at, :] = dot(actc[:, at], dc[...], 0, 0).astype(BF16)

    @pl.loop(1, chips)
    def _(i):
        home(i).wait_recv()

    hot = one_hot()
    hot16 = jnp.where(hot, 1.0, 0.0).astype(BF16)
    back = fin[...].astype(F32)
    left = back[:, :rows].reshape(chips * rows, half).astype(BF16)
    right = back[:, rows:].reshape(chips * rows, half).astype(BF16)
    in_ref[:, :half] = dot(hot16, left, 0, 0).astype(BF16)
    in_ref[:, half:] = dot(hot16, right, 0, 0).astype(BF16)
    col = jnp.sum(
        jnp.where(eye, back[:, cap : cap + 1, :128], 0.0), axis=2, keepdims=True
    ).reshape(chips * rows, 1)
    gate_ref[...] = jnp.sum(jnp.where(hot, col, 0.0), axis=0, keepdims=True).astype(BF16)

    for j in range(1, dps):
        kk = other(j)

        @pl.loop(0, tiles)
        def _(m):
            up_send(j, m, kk, j - 1).wait_recv()

        upg_ref[:, pl.ds(pl.multiple_of(kk * hq, hq), hq)] = ugr[j - 1]

    @pl.loop(0, chips)
    def _(i):
        @pl.when(i > 0)
        def _():
            ici(i).wait_send()
            home(i).wait_send()

        for kk in range(dps):
            side(i, c, kk).wait_send()
            half_sum(i, kk).wait_send()
        for j in range(1, dps):
            cross(i, other(j), k).wait_send()
            cross_sum(i, other(j), dps - 1 - j).wait_send()

    for j in range(1, dps):
        @pl.loop(0, tiles)
        def _(m):
            up_send(j, m, other(j), dps - 1 - j).wait_send()


def on_device(tokens_in, out_grad, gates, expert_ids, slot_ids, w_up, w_down):
    chips = lax.axis_size("expert") // 2
    dps = lax.axis_size("dp")
    tokens, width = tokens_in.shape
    hidden = w_up.shape[2]
    cap = 9 * tokens // (8 * chips)
    rows = (cap + 1 + 7) // 8 * 8
    hq = hidden // dps
    dblk = width // dps
    g = lax.axis_index("expert") // 2
    place = (jnp.bitwise_xor(expert_ids, g) * rows + slot_ids).reshape(1, tokens)
    slots = 2 * dps * chips * rows
    tiles = dblk // min(256, dblk)
    vmem = pl.BlockSpec(memory_space=pltpu.VMEM)
    hbm = pl.BlockSpec(memory_space=pl.ANY)
    dma = pltpu.SemaphoreType.DMA
    in_grad, gate_grad, up_grad, down_grad = pl.pallas_call(
        functools.partial(kernel, chips, dps, cap, rows),
        out_shape=(
            jax.ShapeDtypeStruct((tokens, width), BF16),
            jax.ShapeDtypeStruct((1, tokens), BF16),
            jax.ShapeDtypeStruct((dblk, hidden), BF16),
            jax.ShapeDtypeStruct((hq, width), BF16),
        ),
        in_specs=[vmem] * 4 + [hbm] * 2,
        out_specs=(vmem,) * 4,
        scratch_shapes=[
            pltpu.VMEM((chips, 2 * rows, width), BF16),
            pltpu.VMEM((chips, 2, dps, 2 * rows, width), BF16),
            pltpu.VMEM((slots, width), BF16),
            pltpu.VMEM((slots, width), BF16),
            pltpu.VMEM((slots, hq), BF16),
            pltpu.VMEM((slots, hq), BF16),
            pltpu.VMEM((chips, 2, dps, 2 * rows, width // 2), BF16),
            pltpu.VMEM((chips, dps, 2 * rows, width // 2), BF16),
            pltpu.VMEM((chips, dps - 1, 2 * rows, width // 2), BF16),
            pltpu.VMEM((chips, 2 * rows, width // 2), BF16),
            pltpu.VMEM((width, hq), BF16),
            pltpu.VMEM((hq, width), BF16),
            pltpu.VMEM((dps - 1, dblk, hq), BF16),
            pltpu.VMEM((dps - 1, dblk, hq), BF16),
            dma((2,)),
            dma((chips,)),
            dma((chips,)),
            dma((chips, dps)),
            dma((chips, dps)),
            dma((chips, dps)),
            dma((chips, dps)),
            dma((chips, dps)),
            dma((chips, dps)),
            dma((chips, dps)),
            dma((chips, dps)),
            dma((chips,)),
            dma((chips,)),
            dma((dps, tiles)),
            dma((dps, tiles)),
        ],
        compiler_params=pltpu.CompilerParams(
            collective_id=0, has_side_effects=True, vmem_limit_bytes=61 * 1024 * 1024
        ),
    )(place, gates.reshape(1, tokens), tokens_in, out_grad, w_up, w_down)
    return (in_grad, gate_grad.reshape(tokens), up_grad[None], down_grad[None])


def solution(mesh):
    return jax.shard_map(
        on_device,
        mesh=mesh,
        in_specs=(
            P(("expert", "dp"), None),
            P(("expert", "dp"), None),
            P(("expert", "dp")),
            P(("expert", "dp")),
            P(("expert", "dp")),
            P("expert", None, None),
            P("expert", None, None),
        ),
        out_specs=(
            P(("expert", "dp"), None),
            P(("expert", "dp")),
            P("expert", "dp", None),
            P("expert", "dp", None),
        ),
        check_vma=False,
    )
```

```python
import functools

import jax
import jax.numpy as jnp
from jax import lax
from jax.experimental import pallas as pl
from jax.experimental.pallas import tpu as pltpu
from jax.sharding import PartitionSpec as P

F32 = jnp.float32
BF16 = jnp.bfloat16


def xor(a, b, count):
    total, bit = 0, 1
    while bit < count:
        total = total + lax.rem(a // bit + b // bit, 2) * bit
        bit *= 2
    return total


def gelu_parts(hidden):
    cdf = 0.5 * (1.0 + lax.erf(hidden * 0.7071067811865476))
    pdf = jnp.exp(-0.5 * hidden * hidden) * 0.3989422804014327
    return (hidden * cdf, cdf + hidden * pdf)


def dot(a, b, da, db):
    return lax.dot_general(a, b, (((da,), (db,)), ((), ())), preferred_element_type=F32)


def kernel(
    chips, dps, cap, rows,
    ids_ref, slots_ref, gates_ref, tok_hbm, cot_hbm, up_hbm, down_hbm,
    in_hbm, gate_ref, upg_hbm, downg_hbm,
    tok_ref, cot_ref, in_buf, up_buf, down_buf, tx, rx, xc, dc, actc, dhc, part, sib, xr, fin, wu, wd, ugs,
    w_sem, out_sem, ici_s, ici_r, sf_s, sf_r, xf_s, xf_r, ps_s, ps_r, xr_s, xr_r, fin_s, fin_r, ug_s, ug_r,
):
    me = lax.axis_index("expert")
    k = lax.axis_index("dp")
    g = me // 2
    c = lax.rem(me, 2)
    o = 1 - c
    width = tok_ref.shape[1]
    half = width // 2
    hq = wu.shape[1]
    dblk = width // dps
    per = 2 * dps * rows

    def dev(chip, core, dp):
        return {"expert": chip * 2 + core, "dp": dp}

    def other(j):
        return lax.rem(k + j, dps)

    def remote(src, dst, s, r, target):
        return pltpu.make_async_remote_copy(
            src_ref=src, dst_ref=dst, send_sem=s, recv_sem=r,
            device_id=target, device_id_type=pl.DeviceIdType.MESH,
        )

    def apart(p):
        return p // 2 + lax.rem(p, 2) * (chips // 2)

    def partner(p):
        return xor(g, apart(p), chips)

    def ici(i):
        return remote(tx.at[i], rx.at[i, c, k], ici_s.at[i], ici_r.at[i], dev(partner(i), c, k))

    def side(i, core, kk):
        return remote(
            rx.at[i, core, kk], rx.at[i, core, kk], sf_s.at[i, kk], sf_r.at[i, kk], dev(g, o, k)
        )

    def cross(i, kk, slot):
        return remote(
            rx.at[i, c, slot], rx.at[i, c, slot], xf_s.at[i, kk], xf_r.at[i, slot], dev(g, c, kk)
        )

    def half_sum(i, kk):
        return remote(part.at[i, o, kk], sib.at[i, kk], ps_s.at[i, kk], ps_r.at[i, kk], dev(g, o, k))

    def cross_sum(i, kk, slot):
        return remote(
            part.at[i, c, kk], xr.at[i, slot], xr_s.at[i, kk], xr_r.at[i, slot], dev(g, c, kk)
        )

    def home(i):
        return remote(part.at[i, c, k], fin.at[i], fin_s.at[i], fin_r.at[i], dev(partner(i), c, k))

    tile = min(256, dblk)
    tiles = dblk // tile

    def up_send(j, m, kk, slot, col):
        return remote(
            ugs.at[j - 1, pl.ds(m * tile, tile)],
            upg_hbm.at[pl.ds(m * tile, tile), pl.ds(pl.multiple_of(col * hq, hq), hq)],
            ug_s.at[kk, m], ug_r.at[slot, m], dev(g, c, kk),
        )

    load_up = pltpu.make_async_copy(
        up_hbm.at[0, :, pl.ds(pl.multiple_of(k * hq, hq), hq)], wu, w_sem.at[0]
    )
    load_down = pltpu.make_async_copy(
        down_hbm.at[0, pl.ds(pl.multiple_of(k * hq, hq), hq), :], wd, w_sem.at[1]
    )
    load_tok = pltpu.make_async_copy(tok_hbm, tok_ref, w_sem.at[2])
    load_cot = pltpu.make_async_copy(cot_hbm, cot_ref, w_sem.at[3])
    load_tok.start()
    load_cot.start()
    load_up.start()
    load_down.start()

    barrier = pltpu.get_barrier_semaphore()

    def greet(target):
        pl.semaphore_signal(barrier, inc=1, device_id=target, device_id_type=pl.DeviceIdType.MESH)

    @pl.loop(1, chips)
    def _(i):
        greet(dev(partner(i), c, k))

    greet(dev(g, o, k))
    for j in range(1, dps):
        greet(dev(g, c, other(j)))

    eye = lax.broadcasted_iota(jnp.int32, (1, rows, 128), 1) == lax.broadcasted_iota(
        jnp.int32, (1, rows, 128), 2
    )
    at_cap = lax.broadcasted_iota(jnp.int32, (1, rows, 128), 1) == cap

    def one_hot():
        place = ids_ref[...] * rows + slots_ref[...]
        row = lax.broadcasted_iota(jnp.int32, (rows, place.shape[1]), 0)
        blocks = [jnp.where(place - partner(i) * rows == row, 1.0, 0.0) for i in range(chips)]
        return jnp.concatenate(blocks, axis=0)

    hot = one_hot()
    hot16 = hot.astype(BF16)
    gates = gates_ref[...].astype(F32).reshape(1, -1)
    gate_col = jnp.sum(hot * gates, axis=1, keepdims=True)
    load_tok.wait()
    load_cot.wait()
    gate_row = jnp.sum(jnp.where(eye, gate_col.reshape(chips, rows, 1), 0.0), axis=1, keepdims=True)
    x_pack = dot(hot16, tok_ref[...], 1, 0).reshape(chips, rows, width)
    g_pack = dot(hot16, cot_ref[...], 1, 0).reshape(chips, rows, width)
    first = jnp.where(at_cap, gate_row, x_pack[:, :, :128])
    x_pack = jnp.concatenate([first, x_pack[:, :, 128:]], axis=2)
    both = jnp.concatenate([x_pack, g_pack], axis=1).astype(BF16)
    tx[...] = both
    rx[0, c, k] = both[0]

    pl.semaphore_wait(barrier, chips - 1 + 1 + dps - 1)

    @pl.loop(1, chips)
    def _(i):
        ici(i).start()

    def stage_a(i):
        @pl.when(i > 0)
        def _():
            ici(i).wait_recv()

        for j in range(1, dps):
            cross(i, other(j), k).start()
        side(i, c, k).start()

    def stage_b(i):
        for j in range(1, dps):
            cross(i, other(j), other(j)).wait_recv()
            side(i, c, other(j)).start()

    def stage_c(i):
        for kk in range(dps):
            side(i, o, kk).wait_recv()
        blk = rx[i].reshape(2 * dps, 2 * rows, width).astype(F32)
        x = blk[:, :rows].reshape(per, width).astype(BF16)
        cot = blk[:, rows:].reshape(per, width)
        gate = jnp.sum(
            jnp.where(eye, blk[:, cap : cap + 1, :128], 0.0), axis=2, keepdims=True
        ).reshape(per, 1)
        at = pl.ds(pl.multiple_of(i * per, per), per)
        xc[at, :] = x
        dc[at, :] = (gate * cot).astype(BF16)
        hidden = dot(x, wu[...], 1, 0)
        gv = dot(cot.astype(BF16), wd[...], 1, 1)
        value, slope = gelu_parts(hidden)
        act = value.astype(BF16)
        dh = (gate * gv * slope).astype(BF16)
        actc[at, :] = act
        dhc[at, :] = dh
        gp = jnp.sum(act.astype(F32) * gv, axis=1, keepdims=True).reshape(2 * dps, rows, 1)
        gp_row = jnp.sum(jnp.where(eye, gp, 0.0), axis=1, keepdims=True)
        d = dot(dh, wu[...], 1, 1).reshape(2 * dps, rows, width)
        lead = jnp.where(at_cap, gp_row, d[:, :, :128])
        left = jnp.concatenate([lead, d[:, :, 128:half]], axis=2)
        whole = jnp.concatenate([left, d[:, :, half:]], axis=1).astype(BF16)
        part[i] = whole.reshape(2, dps, 2 * rows, half)
        for kk in range(dps):
            half_sum(i, kk).start()

    def stage_d(i):
        for j in list(range(1, dps)) + [0]:
            kk = other(j)
            half_sum(i, kk).wait_recv()
            part[i, c, kk] = (part[i, c, kk].astype(F32) + sib[i, kk].astype(F32)).astype(BF16)

    def stage_x(i):
        for j in range(1, dps):
            cross_sum(i, other(j), dps - 1 - j).start()

    def stage_e(i):
        total = part[i, c, k].astype(F32)
        for j in range(1, dps):
            cross_sum(i, other(j), j - 1).wait_recv()
            total = total + xr[i, j - 1].astype(F32)
        total = total.astype(BF16)

        @pl.when(i > 0)
        def _():
            part[i, c, k] = total
            home(i).start()

        @pl.when(i == 0)
        def _():
            fin[0] = total

    load_up.wait()
    load_down.wait()

    @pl.loop(0, chips + 2)
    def _(t):
        @pl.when(t < chips)
        def _():
            stage_a(t)

        @pl.when(t == chips - 1)
        def _():
            pl.loop(0, chips - 4)(stage_x)

        @pl.when(t >= chips)
        def _():
            stage_x(t - 4)

        @pl.when(jnp.logical_and(t >= 1, t < chips + 1))
        def _():
            stage_b(t - 1)

        @pl.when(t >= 2)
        def _():
            stage_c(t - 2)

        @pl.when(t >= 3)
        def _():
            stage_d(t - 3)

    stage_x(chips - 2)
    stage_d(chips - 1)
    stage_x(chips - 1)

    def up_tile(kk, m):
        at = pl.ds(pl.multiple_of(kk * dblk + m * tile, tile), tile)
        return dot(xc[:, at], dhc[...], 0, 0).astype(BF16)

    for j in range(1, dps):
        @pl.loop(0, tiles)
        def _(m):
            ugs[j - 1, pl.ds(pl.multiple_of(m * tile, tile), tile), :] = up_tile(other(j), m)
            up_send(j, m, other(j), dps - 1 - j, k).start()

    pl.loop(0, chips // 2)(stage_e)

    @pl.loop(0, tiles)
    def _(m):
        up_buf[pl.ds(pl.multiple_of(m * tile, tile), tile), :] = up_tile(k, m)

    mine = pl.ds(pl.multiple_of(k * hq, hq), hq)
    put_up = pltpu.make_async_copy(up_buf, upg_hbm.at[:, mine], out_sem.at[0])
    put_up.start()
    dtile = min(256, hq)

    @pl.loop(0, hq // dtile)
    def _(m):
        at = pl.ds(pl.multiple_of(m * dtile, dtile), dtile)
        down_buf[at, :] = dot(actc[:, at], dc[...], 0, 0).astype(BF16)

    put_down = pltpu.make_async_copy(down_buf, downg_hbm, out_sem.at[1])
    put_down.start()
    pl.loop(chips // 2, chips)(stage_e)

    @pl.loop(1, chips)
    def _(i):
        home(i).wait_recv()

    hot = one_hot()
    hot16 = hot.astype(BF16)
    back = fin[...].astype(F32)
    left = back[:, :rows].reshape(chips * rows, half).astype(BF16)
    right = back[:, rows:].reshape(chips * rows, half).astype(BF16)
    in_buf[:, :half] = dot(hot16, left, 0, 0).astype(BF16)
    in_buf[:, half:] = dot(hot16, right, 0, 0).astype(BF16)
    col = jnp.sum(
        jnp.where(eye, back[:, cap : cap + 1, :128], 0.0), axis=2, keepdims=True
    ).reshape(chips * rows, 1)
    gate_ref[...] = jnp.sum(hot * col, axis=0).astype(BF16)
    put_in = pltpu.make_async_copy(in_buf, in_hbm, out_sem.at[2])
    put_in.start()

    for j in range(1, dps):
        kk = other(j)

        @pl.loop(0, tiles)
        def _(m):
            up_send(j, m, kk, j - 1, kk).wait_recv()

    @pl.loop(0, chips)
    def _(i):
        @pl.when(i > 0)
        def _():
            ici(i).wait_send()
            home(i).wait_send()

        for kk in range(dps):
            side(i, c, kk).wait_send()
            half_sum(i, kk).wait_send()
        for j in range(1, dps):
            cross(i, other(j), k).wait_send()
            cross_sum(i, other(j), dps - 1 - j).wait_send()

    for j in range(1, dps):
        @pl.loop(0, tiles)
        def _(m):
            up_send(j, m, other(j), dps - 1 - j, k).wait_send()

    put_up.wait()
    put_down.wait()
    put_in.wait()


def hand_on(*refs):
    count = len(refs) // 2
    copies = [
        pltpu.make_async_copy(refs[n], refs[count + n], refs[-1].at[n]) for n in range(count)
    ]
    for copy in copies:
        copy.start()
    for copy in copies:
        copy.wait()


def on_device(tokens_in, out_grad, gates, expert_ids, slot_ids, w_up, w_down):
    chips = lax.axis_size("expert") // 2
    dps = lax.axis_size("dp")
    tokens, width = tokens_in.shape
    hidden = w_up.shape[2]
    cap = 9 * tokens // (8 * chips)
    rows = (cap + 1 + 7) // 8 * 8
    hq = hidden // dps
    dblk = width // dps
    slots = 2 * dps * chips * rows
    tiles = dblk // min(256, dblk)
    vmem = pl.BlockSpec(memory_space=pltpu.VMEM)
    hbm = pl.BlockSpec(memory_space=pl.ANY)
    dma = pltpu.SemaphoreType.DMA
    raw = pl.pallas_call(
        functools.partial(kernel, chips, dps, cap, rows),
        out_shape=(
            jax.ShapeDtypeStruct((tokens, width), BF16),
            jax.ShapeDtypeStruct((tokens,), BF16),
            jax.ShapeDtypeStruct((dblk, hidden), BF16),
            jax.ShapeDtypeStruct((hq, width), BF16),
        ),
        in_specs=[vmem] * 3 + [hbm] * 4,
        out_specs=(hbm, vmem, hbm, hbm),
        scratch_shapes=[
            pltpu.VMEM((tokens, width), BF16),
            pltpu.VMEM((tokens, width), BF16),
            pltpu.VMEM((tokens, width), BF16),
            pltpu.VMEM((dblk, hq), BF16),
            pltpu.VMEM((hq, width), BF16),
            pltpu.VMEM((chips, 2 * rows, width), BF16),
            pltpu.VMEM((chips, 2, dps, 2 * rows, width), BF16),
            pltpu.VMEM((slots, width), BF16),
            pltpu.VMEM((slots, width), BF16),
            pltpu.VMEM((slots, hq), BF16),
            pltpu.VMEM((slots, hq), BF16),
            pltpu.VMEM((chips, 2, dps, 2 * rows, width // 2), BF16),
            pltpu.VMEM((chips, dps, 2 * rows, width // 2), BF16),
            pltpu.VMEM((chips, dps - 1, 2 * rows, width // 2), BF16),
            pltpu.VMEM((chips, 2 * rows, width // 2), BF16),
            pltpu.VMEM((width, hq), BF16),
            pltpu.VMEM((hq, width), BF16),
            pltpu.VMEM((dps - 1, dblk, hq), BF16),
            dma((4,)),
            dma((3,)),
            dma((chips,)),
            dma((chips,)),
            dma((chips, dps)),
            dma((chips, dps)),
            dma((chips, dps)),
            dma((chips, dps)),
            dma((chips, dps)),
            dma((chips, dps)),
            dma((chips, dps)),
            dma((chips, dps)),
            dma((chips,)),
            dma((chips,)),
            dma((dps, tiles)),
            dma((dps, tiles)),
        ],
        compiler_params=pltpu.CompilerParams(
            collective_id=0, has_side_effects=True, vmem_limit_bytes=61 * 1024 * 1024
        ),
    )(
        expert_ids.reshape(1, tokens), slot_ids.reshape(1, tokens), gates,
        tokens_in, out_grad, w_up, w_down,
    )
    in_grad, gate_grad, up_grad, down_grad = pl.pallas_call(
        hand_on,
        out_shape=[jax.ShapeDtypeStruct(r.shape, r.dtype) for r in raw],
        in_specs=[hbm] * 4,
        out_specs=[hbm] * 4,
        scratch_shapes=[dma((4,))],
    )(*raw)
    return (in_grad, gate_grad, up_grad[None], down_grad[None])


def solution(mesh):
    return jax.shard_map(
        on_device,
        mesh=mesh,
        in_specs=(
            P(("expert", "dp"), None),
            P(("expert", "dp"), None),
            P(("expert", "dp")),
            P(("expert", "dp")),
            P(("expert", "dp")),
            P("expert", None, None),
            P("expert", None, None),
        ),
        out_specs=(
            P(("expert", "dp"), None),
            P(("expert", "dp")),
            P("expert", "dp", None),
            P("expert", "dp", None),
        ),
        check_vma=False,
    )
```

```python
import functools

import jax
import jax.numpy as jnp
from jax import lax
from jax.experimental import pallas as pl
from jax.experimental.pallas import tpu as pltpu
from jax.sharding import PartitionSpec as P

F32 = jnp.float32
BF16 = jnp.bfloat16


def xor(a, b, count):
    total, bit = 0, 1
    while bit < count:
        total = total + lax.rem(a // bit + b // bit, 2) * bit
        bit *= 2
    return total


def gelu_parts(hidden):
    cdf = 0.5 * (1.0 + lax.erf(hidden * 0.7071067811865476))
    pdf = jnp.exp(-0.5 * hidden * hidden) * 0.3989422804014327
    return (hidden * cdf, cdf + hidden * pdf)


def dot(a, b, da, db):
    return lax.dot_general(a, b, (((da,), (db,)), ((), ())), preferred_element_type=F32)


def kernel(
    chips, dps, cap, rows,
    ids_ref, slots_ref, gates_ref, tok_hbm, cot_hbm, up_hbm, down_hbm,
    in_hbm, gate_ref, upg_hbm, downg_hbm,
    tok_ref, cot_ref, in_buf, up_buf, down_buf, tx, rx, xc, dc, actc, dhc, act_tmp, dh_tmp,
    part, sib, fin, wu, wd, ugs,
    w_sem, out_sem, ici_s, ici_r, sf_s, sf_r, xf_s, xf_r, ps_s, ps_r, fin_s, fin_r, ug_s, ug_r,
):
    me = lax.axis_index("expert")
    k = lax.axis_index("dp")
    g = me // 2
    c = lax.rem(me, 2)
    o = 1 - c
    tokens, width = tok_ref.shape
    half = width // 2
    hidden_dev = wu.shape[1]
    hq = hidden_dev // dps
    dblk = width // dps
    full = rows - 8
    pairs = chips // 2
    own_per = 4 * rows
    other_per = own_per * (dps - 1)
    mine = pl.ds(pl.multiple_of(k * hq, hq), hq)

    def dev(chip, core, dp):
        return {"expert": chip * 2 + core, "dp": dp}

    def other(j):
        return lax.rem(k + j, dps)

    def remote(src, dst, s, r, target):
        return pltpu.make_async_remote_copy(
            src_ref=src, dst_ref=dst, send_sem=s, recv_sem=r,
            device_id=target, device_id_type=pl.DeviceIdType.MESH,
        )

    def partner(p):
        return xor(g, p // 2 + lax.rem(p, 2) * (chips // 2), chips)

    def ici(i):
        return remote(tx.at[i], rx.at[k, i, c], ici_s.at[i], ici_r.at[i], dev(partner(i), c, k))

    def side(i, core, kk):
        return remote(
            rx.at[kk, i, core], rx.at[kk, i, core], sf_s.at[i, kk], sf_r.at[i, kk], dev(g, o, k)
        )

    def cross(i, kk, slot):
        return remote(
            rx.at[slot, i, c], rx.at[slot, i, c], xf_s.at[i, kk], xf_r.at[i, slot], dev(g, c, kk)
        )

    def half_sum(i):
        return remote(part.at[i, o], sib.at[i], ps_s.at[i], ps_r.at[i], dev(g, o, k))

    def home(i):
        return remote(part.at[i, c], fin.at[i], fin_s.at[i], fin_r.at[i], dev(partner(i), c, k))

    tile = min(256, dblk)
    tiles = dblk // tile

    def up_send(j, m, kk, slot, col):
        return remote(
            ugs.at[j - 1, pl.ds(m * tile, tile)],
            upg_hbm.at[pl.ds(m * tile, tile), pl.ds(pl.multiple_of(col * hq, hq), hq)],
            ug_s.at[kk, m], ug_r.at[slot, m], dev(g, c, kk),
        )

    load_tok = pltpu.make_async_copy(tok_hbm, tok_ref, w_sem.at[2])
    load_cot = pltpu.make_async_copy(cot_hbm, cot_ref, w_sem.at[3])
    load_up = pltpu.make_async_copy(up_hbm.at[0], wu, w_sem.at[0])
    load_down = pltpu.make_async_copy(down_hbm.at[0], wd, w_sem.at[1])
    load_tok.start()
    load_cot.start()
    load_up.start()
    load_down.start()

    barrier = pltpu.get_barrier_semaphore()

    def greet(target):
        pl.semaphore_signal(barrier, inc=1, device_id=target, device_id_type=pl.DeviceIdType.MESH)

    @pl.loop(1, chips)
    def _(i):
        greet(dev(partner(i), c, k))

    greet(dev(g, o, k))
    for j in range(1, dps):
        greet(dev(g, c, other(j)))

    eye = lax.broadcasted_iota(jnp.int32, (1, rows, 128), 1) == lax.broadcasted_iota(
        jnp.int32, (1, rows, 128), 2
    )
    at_cap = lax.broadcasted_iota(jnp.int32, (1, rows, 128), 1) == cap
    upper = lax.broadcasted_iota(jnp.int32, (1, 8, 1), 1) < 4

    def one_hot():
        place = ids_ref[...] * rows + slots_ref[...]
        row = lax.broadcasted_iota(jnp.int32, (rows, place.shape[1]), 0)
        blocks = [jnp.where(place - partner(i) * rows == row, 1.0, 0.0) for i in range(chips)]
        return jnp.concatenate(blocks, axis=0)

    def rolled(tiles8, shift):
        count = tiles8.shape[0]
        flat = pltpu.roll(tiles8.reshape(count * 8, width), shift, 0)
        return flat.reshape(count, 8, width)

    hot = one_hot()
    hot16 = hot.astype(BF16)
    gates = gates_ref[...].astype(F32).reshape(1, -1)
    gate_col = jnp.sum(hot * gates, axis=1, keepdims=True)
    load_tok.wait()
    load_cot.wait()
    x_pack = dot(hot16, tok_ref[...], 1, 0).reshape(chips, rows, width)
    d_pack = (dot(hot16, cot_ref[...], 1, 0) * gate_col).reshape(chips, rows, width)
    mixed = jnp.where(upper, x_pack[:, full:], rolled(d_pack[:, full:], 4))
    both = jnp.concatenate([x_pack[:, :full], mixed, d_pack[:, :full]], axis=1).astype(BF16)
    tx[...] = both
    rx[k, 0, c] = both[0]

    pl.semaphore_wait(barrier, chips - 1 + 1 + dps - 1)

    @pl.loop(1, chips)
    def _(i):
        ici(i).start()

    def stage_a(i):
        @pl.when(i > 0)
        def _():
            ici(i).wait_recv()

        for j in range(1, dps):
            cross(i, other(j), k).start()
        side(i, c, k).start()

    def stage_b(i):
        for j in range(1, dps):
            cross(i, other(j), other(j)).wait_recv()
            side(i, c, other(j)).start()

    def unpack(blk):
        blk = blk.astype(F32)
        count = blk.shape[0]
        mid = blk[:, full : full + 8]
        x_last = jnp.where(upper, mid, 0.0)
        d_last = jnp.where(upper, rolled(mid, count * 8 - 4), 0.0)
        x = jnp.concatenate([blk[:, :full], x_last], axis=1)
        d = jnp.concatenate([blk[:, full + 8 :], d_last], axis=1)
        return (
            x.reshape(count * rows, width).astype(BF16),
            d.reshape(count * rows, width).astype(BF16),
        )

    def stage_c(t):
        side(2 * t, o, k).wait_recv()
        side(2 * t + 1, o, k).wait_recv()
        x, d = unpack(rx[k, pl.ds(2 * t, 2)].reshape(4, 2 * full + 8, width))
        at = pl.ds(pl.multiple_of(t * own_per, own_per), own_per)
        xc[at, :] = x
        dc[at, :] = d
        value, slope = gelu_parts(dot(x, wu[...], 1, 0))
        d_act = dot(d, wd[...], 1, 1)
        act = value.astype(BF16)
        dh = (d_act * slope).astype(BF16)
        act_tmp[...] = act
        dh_tmp[...] = dh
        actc[at, :] = act_tmp[:, mine]
        dhc[at, :] = dh_tmp[:, mine]
        gp = jnp.sum(act.astype(F32) * d_act, axis=1, keepdims=True).reshape(4, rows, 1)
        gp_row = jnp.sum(jnp.where(eye, gp, 0.0), axis=1, keepdims=True)
        d_in = dot(dh, wu[...], 1, 1).reshape(4, rows, width)
        lead = jnp.where(at_cap, gp_row, d_in[:, :, :128])
        left = jnp.concatenate([lead, d_in[:, :, 128:half]], axis=2)
        whole = jnp.concatenate([left, d_in[:, :, half:]], axis=1).astype(BF16)
        part[pl.ds(2 * t, 2)] = whole.reshape(2, 2, 2 * rows, half)
        half_sum(2 * t).start()
        half_sum(2 * t + 1).start()

    def stage_o(t):
        for j in range(1, dps):
            kk = other(j)
            side(2 * t, o, kk).wait_recv()
            side(2 * t + 1, o, kk).wait_recv()
            x, d = unpack(rx[kk, pl.ds(2 * t, 2)].reshape(4, 2 * full + 8, width))
            at = pl.ds(
                pl.multiple_of(pairs * own_per + t * other_per + (j - 1) * own_per, own_per), own_per
            )
            xc[at, :] = x
            dc[at, :] = d
            value, slope = gelu_parts(dot(x, wu[:, mine], 1, 0))
            d_act = dot(d, wd[mine, :], 1, 1)
            actc[at, :] = value.astype(BF16)
            dhc[at, :] = (d_act * slope).astype(BF16)

    def stage_e(i):
        half_sum(i).wait_recv()
        total = (part[i, c].astype(F32) + sib[i].astype(F32)).astype(BF16)

        @pl.when(i > 0)
        def _():
            part[i, c] = total
            home(i).start()

        @pl.when(i == 0)
        def _():
            fin[0] = total

    stage_a(0)
    load_up.wait()
    load_down.wait()

    @pl.loop(0, pairs)
    def _(t):
        @pl.when(t > 0)
        def _():
            stage_a(2 * t)

        stage_a(2 * t + 1)

        @pl.when(t >= 1)
        def _():
            stage_c(t - 1)
            stage_b(2 * t - 2)
            stage_b(2 * t - 1)

        @pl.when(t >= 2)
        def _():
            stage_o(t - 2)

    pl.loop(0, chips - 2)(stage_e)
    stage_c(pairs - 1)
    stage_b(chips - 2)
    stage_b(chips - 1)
    stage_o(pairs - 2)
    stage_e(chips - 2)
    stage_e(chips - 1)
    stage_o(pairs - 1)

    def up_tile(kk, m):
        at = pl.ds(pl.multiple_of(kk * dblk + m * tile, tile), tile)
        return dot(xc[:, at], dhc[...], 0, 0).astype(BF16)

    for j in range(1, dps):
        @pl.loop(0, tiles)
        def _(m):
            ugs[j - 1, pl.ds(pl.multiple_of(m * tile, tile), tile), :] = up_tile(other(j), m)
            up_send(j, m, other(j), dps - 1 - j, k).start()

    @pl.loop(0, tiles)
    def _(m):
        up_buf[pl.ds(pl.multiple_of(m * tile, tile), tile), :] = up_tile(k, m)

    put_up = pltpu.make_async_copy(up_buf, upg_hbm.at[:, mine], out_sem.at[0])
    put_up.start()
    dtile = min(256, hq)

    @pl.loop(0, hq // dtile)
    def _(m):
        at = pl.ds(pl.multiple_of(m * dtile, dtile), dtile)
        down_buf[at, :] = dot(actc[:, at], dc[...], 0, 0).astype(BF16)

    put_down = pltpu.make_async_copy(down_buf, downg_hbm, out_sem.at[1])
    put_down.start()

    @pl.loop(1, chips)
    def _(i):
        home(i).wait_recv()

    hot = one_hot()
    hot16 = hot.astype(BF16)
    back = fin[...].astype(F32)
    left = back[:, :rows].reshape(chips * rows, half).astype(BF16)
    right = back[:, rows:].reshape(chips * rows, half).astype(BF16)
    in_buf[:, :half] = dot(hot16, left, 0, 0).astype(BF16)
    in_buf[:, half:] = dot(hot16, right, 0, 0).astype(BF16)
    put_in = pltpu.make_async_copy(in_buf, in_hbm, out_sem.at[2])
    put_in.start()
    col = jnp.sum(
        jnp.where(eye, back[:, cap : cap + 1, :128], 0.0), axis=2, keepdims=True
    ).reshape(chips * rows, 1)
    scaled = jnp.sum(hot * col, axis=0, keepdims=True)
    gate_ref[...] = (scaled / gates_ref[...].astype(F32).reshape(1, -1)).astype(BF16).reshape(tokens)

    @pl.loop(0, chips)
    def _(i):
        @pl.when(i > 0)
        def _():
            ici(i).wait_send()
            home(i).wait_send()

        half_sum(i).wait_send()
        for kk in range(dps):
            side(i, c, kk).wait_send()
        for j in range(1, dps):
            cross(i, other(j), k).wait_send()

    for j in range(1, dps):
        kk = other(j)

        @pl.loop(0, tiles)
        def _(m):
            up_send(j, m, kk, j - 1, kk).wait_recv()
            up_send(j, m, kk, dps - 1 - j, k).wait_send()

    put_up.wait()
    put_down.wait()
    put_in.wait()


def hand_on(a, b, c, d, a_out, b_out, c_out, d_out, a_buf, b_buf, c_buf, d_buf, sems):
    buffers = (a_buf, b_buf, c_buf, d_buf)
    ins = [
        pltpu.make_async_copy(ref, buf, sems.at[0, n])
        for n, (ref, buf) in enumerate(zip((a, b, c, d), buffers))
    ]
    outs = [
        pltpu.make_async_copy(buf, ref, sems.at[1, n])
        for n, (ref, buf) in enumerate(zip((a_out, b_out, c_out, d_out), buffers))
    ]
    for copy in ins:
        copy.start()
    for first, then in zip(ins, outs):
        first.wait()
        then.start()
    for copy in outs:
        copy.wait()


def on_device(tokens_in, out_grad, gates, expert_ids, slot_ids, w_up, w_down):
    chips = lax.axis_size("expert") // 2
    dps = lax.axis_size("dp")
    tokens, width = tokens_in.shape
    hidden = w_up.shape[2]
    cap = 9 * tokens // (8 * chips)
    assert 1 <= cap % 8 <= 4
    rows = cap // 8 * 8 + 8
    hq = hidden // dps
    dblk = width // dps
    slots = 2 * dps * chips * rows
    tiles = dblk // min(256, dblk)
    vmem = pl.BlockSpec(memory_space=pltpu.VMEM)
    hbm = pl.BlockSpec(memory_space=pl.ANY)
    dma = pltpu.SemaphoreType.DMA
    raw = pl.pallas_call(
        functools.partial(kernel, chips, dps, cap, rows),
        out_shape=(
            jax.ShapeDtypeStruct((tokens, width), BF16),
            jax.ShapeDtypeStruct((tokens,), BF16),
            jax.ShapeDtypeStruct((dblk, hidden), BF16),
            jax.ShapeDtypeStruct((hq, width), BF16),
        ),
        in_specs=[vmem] * 3 + [hbm] * 4,
        out_specs=(hbm, vmem, hbm, hbm),
        scratch_shapes=[
            pltpu.VMEM((tokens, width), BF16),
            pltpu.VMEM((tokens, width), BF16),
            pltpu.VMEM((tokens, width), BF16),
            pltpu.VMEM((dblk, hq), BF16),
            pltpu.VMEM((hq, width), BF16),
            pltpu.VMEM((chips, 2 * rows - 8, width), BF16),
            pltpu.VMEM((dps, chips, 2, 2 * rows - 8, width), BF16),
            pltpu.VMEM((slots, width), BF16),
            pltpu.VMEM((slots, width), BF16),
            pltpu.VMEM((slots, hq), BF16),
            pltpu.VMEM((slots, hq), BF16),
            pltpu.VMEM((4 * rows, hidden), BF16),
            pltpu.VMEM((4 * rows, hidden), BF16),
            pltpu.VMEM((chips, 2, 2 * rows, width // 2), BF16),
            pltpu.VMEM((chips, 2 * rows, width // 2), BF16),
            pltpu.VMEM((chips, 2 * rows, width // 2), BF16),
            pltpu.VMEM((width, hidden), BF16),
            pltpu.VMEM((hidden, width), BF16),
            pltpu.VMEM((dps - 1, dblk, hq), BF16),
            dma((4,)),
            dma((3,)),
            dma((chips,)),
            dma((chips,)),
            dma((chips, dps)),
            dma((chips, dps)),
            dma((chips, dps)),
            dma((chips, dps)),
            dma((chips,)),
            dma((chips,)),
            dma((chips,)),
            dma((chips,)),
            dma((dps, tiles)),
            dma((dps, tiles)),
        ],
        compiler_params=pltpu.CompilerParams(
            collective_id=0, has_side_effects=True, vmem_limit_bytes=61 * 1024 * 1024
        ),
    )(
        expert_ids.reshape(1, tokens), slot_ids.reshape(1, tokens), gates,
        tokens_in, out_grad, w_up, w_down,
    )
    in_grad, gate_grad, up_grad, down_grad = pl.pallas_call(
        hand_on,
        out_shape=[jax.ShapeDtypeStruct(r.shape, r.dtype) for r in raw],
        in_specs=[hbm] * 4,
        out_specs=[hbm] * 4,
        scratch_shapes=[pltpu.VMEM(r.shape, r.dtype) for r in raw] + [dma((2, 4))],
    )(*raw)
    return (in_grad, gate_grad, up_grad[None], down_grad[None])


def solution(mesh):
    return jax.shard_map(
        on_device,
        mesh=mesh,
        in_specs=(
            P(("expert", "dp"), None),
            P(("expert", "dp"), None),
            P(("expert", "dp")),
            P(("expert", "dp")),
            P(("expert", "dp")),
            P("expert", None, None),
            P("expert", None, None),
        ),
        out_specs=(
            P(("expert", "dp"), None),
            P(("expert", "dp")),
            P("expert", "dp", None),
            P("expert", "dp", None),
        ),
        check_vma=False,
    )
```

```python
import functools

import jax
import jax.numpy as jnp
from jax import lax
from jax.experimental import pallas as pl
from jax.experimental.pallas import tpu as pltpu
from jax.sharding import PartitionSpec as P

F32 = jnp.float32
BF16 = jnp.bfloat16


def xor(a, b, count):
    total, bit = 0, 1
    while bit < count:
        total = total + lax.rem(a // bit + b // bit, 2) * bit
        bit *= 2
    return total


def gelu_parts(hidden):
    cdf = 0.5 * (1.0 + lax.erf(hidden * 0.7071067811865476))
    pdf = jnp.exp(-0.5 * hidden * hidden) * 0.3989422804014327
    return (hidden * cdf, cdf + hidden * pdf)


def dot(a, b, da, db):
    return lax.dot_general(a, b, (((da,), (db,)), ((), ())), preferred_element_type=F32)


def kernel(
    chips, dps, cap, rows,
    ids_ref, slots_ref, gates_ref, tok_hbm, cot_hbm, up_hbm, down_hbm,
    fin, upg_hbm, downg_hbm,
    tok_ref, cot_ref, up_buf, down_buf, tx, rx, xc, dc, actc, dhc, act_tmp,
    part, sib, wu, wd,
    w_sem, out_sem, ici_s, ici_r, sf_s, sf_r, xf_s, xf_r, ps_s, ps_r, fin_s, fin_r,
):
    me = lax.axis_index("expert")
    k = lax.axis_index("dp")
    g = me // 2
    c = lax.rem(me, 2)
    o = 1 - c
    tokens, width = tok_ref.shape
    half = width // 2
    hidden_dev = wu.shape[1]
    hq = hidden_dev // dps
    dblk = width // dps
    full = rows - 8
    pairs = chips // 2
    own_per = 4 * rows
    other_per = own_per * (dps - 1)
    mine = pl.ds(pl.multiple_of(k * hq, hq), hq)

    def dev(chip, core, dp):
        return {"expert": chip * 2 + core, "dp": dp}

    def other(j):
        return lax.rem(k + j, dps)

    def remote(src, dst, s, r, target):
        return pltpu.make_async_remote_copy(
            src_ref=src, dst_ref=dst, send_sem=s, recv_sem=r,
            device_id=target, device_id_type=pl.DeviceIdType.MESH,
        )

    def partner(p):
        return xor(g, p, chips)

    def ici(i):
        return remote(tx.at[i], rx.at[k, i, c], ici_s.at[i], ici_r.at[i], dev(partner(i), c, k))

    def side(i, core, kk):
        return remote(
            rx.at[kk, i, core], rx.at[kk, i, core], sf_s.at[i, kk], sf_r.at[i, kk], dev(g, o, k)
        )

    def cross(i, kk, slot):
        return remote(
            rx.at[slot, i, c], rx.at[slot, i, c], xf_s.at[i, kk], xf_r.at[i, slot], dev(g, c, kk)
        )

    def half_sum(i):
        return remote(part.at[i, o], sib.at[i], ps_s.at[i], ps_r.at[i], dev(g, o, k))

    def home(i):
        return remote(part.at[i, c], fin.at[i], fin_s.at[i], fin_r.at[i], dev(partner(i), c, k))

    load_tok = pltpu.make_async_copy(tok_hbm, tok_ref, w_sem.at[2])
    load_cot = pltpu.make_async_copy(cot_hbm, cot_ref, w_sem.at[3])
    load_up = pltpu.make_async_copy(up_hbm.at[0], wu, w_sem.at[0])
    load_down = pltpu.make_async_copy(down_hbm.at[0], wd, w_sem.at[1])
    load_tok.start()
    load_cot.start()
    load_up.start()
    load_down.start()

    barrier = pltpu.get_barrier_semaphore()

    def greet(target):
        pl.semaphore_signal(barrier, inc=1, device_id=target, device_id_type=pl.DeviceIdType.MESH)

    @pl.loop(1, chips)
    def _(i):
        greet(dev(partner(i), c, k))

    greet(dev(g, o, k))
    for j in range(1, dps):
        greet(dev(g, c, other(j)))

    eye = lax.broadcasted_iota(jnp.int32, (1, rows, 128), 1) == lax.broadcasted_iota(
        jnp.int32, (1, rows, 128), 2
    )
    at_cap = lax.broadcasted_iota(jnp.int32, (1, rows, 128), 1) == cap
    upper = lax.broadcasted_iota(jnp.int32, (1, 8, 1), 1) < 4

    def rolled(tiles8, shift):
        count = tiles8.shape[0]
        flat = pltpu.roll(tiles8.reshape(count * 8, width), shift, 0)
        return flat.reshape(count, 8, width)

    hot = one_hot(ids_ref, slots_ref, g, chips, rows)
    hot16 = hot.astype(BF16)
    gates = gates_ref[...].astype(F32).reshape(1, -1)
    gate_col = jnp.sum(hot * gates, axis=1, keepdims=True)
    load_tok.wait()
    load_cot.wait()
    x_pack = dot(hot16, tok_ref[...], 1, 0).reshape(chips, rows, width)
    d_pack = (dot(hot16, cot_ref[...], 1, 0) * gate_col).reshape(chips, rows, width)
    mixed = jnp.where(upper, x_pack[:, full:], rolled(d_pack[:, full:], 4))
    both = jnp.concatenate([x_pack[:, :full], mixed, d_pack[:, :full]], axis=1).astype(BF16)
    tx[...] = both
    rx[k, 0, c] = both[0]

    pl.semaphore_wait(barrier, chips - 1 + 1 + dps - 1)

    ici(chips // 2).start()

    @pl.loop(1, chips // 2)
    def _(i):
        ici(i).start()
        ici(chips // 2 + i).start()

    def stage_a(i):
        @pl.when(i > 0)
        def _():
            ici(i).wait_recv()

        for j in range(1, dps):
            cross(i, other(j), k).start()
        side(i, c, k).start()

    def stage_b(i):
        for j in range(1, dps):
            cross(i, other(j), other(j)).wait_recv()
            side(i, c, other(j)).start()

    def unpack(blk):
        blk = blk.astype(F32)
        count = blk.shape[0]
        mid = blk[:, full : full + 8]
        x_last = jnp.where(upper, mid, 0.0)
        d_last = jnp.where(upper, rolled(mid, count * 8 - 4), 0.0)
        x = jnp.concatenate([blk[:, :full], x_last], axis=1)
        d = jnp.concatenate([blk[:, full + 8 :], d_last], axis=1)
        return (
            x.reshape(count * rows, width).astype(BF16),
            d.reshape(count * rows, width).astype(BF16),
        )

    def stage_c(t):
        side(2 * t, o, k).wait_recv()
        side(2 * t + 1, o, k).wait_recv()
        x, d = unpack(rx[k, pl.ds(2 * t, 2)].reshape(4, 2 * full + 8, width))
        at = pl.ds(pl.multiple_of(t * own_per, own_per), own_per)
        xc[at, :] = x
        dc[at, :] = d
        value, slope = gelu_parts(dot(x, wu[...], 1, 0))
        d_act = dot(d, wd[...], 1, 1)
        act = value.astype(BF16)
        dh = (d_act * slope).astype(BF16)
        act_tmp[...] = act
        actc[at, :] = act_tmp[:, mine]
        dhc[at, :] = dh
        gp = jnp.sum(act.astype(F32) * d_act, axis=1, keepdims=True).reshape(4, rows, 1)
        gp_row = jnp.sum(jnp.where(eye, gp, 0.0), axis=1, keepdims=True)
        d_in = dot(dh, wu[...], 1, 1).reshape(4, rows, width)
        lead = jnp.where(at_cap, gp_row, d_in[:, :, :128])
        left = jnp.concatenate([lead, d_in[:, :, 128:half]], axis=2)
        whole = jnp.concatenate([left, d_in[:, :, half:]], axis=1).astype(BF16)
        part[pl.ds(2 * t, 2)] = whole.reshape(2, 2, 2 * rows, half)
        half_sum(2 * t).start()
        half_sum(2 * t + 1).start()

    def stage_o(t):
        for j in range(1, dps):
            kk = other(j)
            side(2 * t, o, kk).wait_recv()
            side(2 * t + 1, o, kk).wait_recv()
            x, d = unpack(rx[kk, pl.ds(2 * t, 2)].reshape(4, 2 * full + 8, width))
            at = pl.ds(
                pl.multiple_of(pairs * own_per + t * other_per + (j - 1) * own_per, own_per), own_per
            )
            xc[at, :] = x
            dc[at, :] = d
            value, slope = gelu_parts(dot(x, wu[...], 1, 0))
            d_act = dot(d, wd[...], 1, 1)
            act_tmp[...] = value.astype(BF16)
            actc[at, :] = act_tmp[:, mine]
            dhc[at, :] = (d_act * slope).astype(BF16)

    def stage_e(i):
        half_sum(i).wait_recv()
        total = (part[i, c].astype(F32) + sib[i].astype(F32)).astype(BF16)

        @pl.when(i > 0)
        def _():
            part[i, c] = total
            home(i).start()

        @pl.when(i == 0)
        def _():
            part[i, c] = total
            put_own.start()

    put_own = pltpu.make_async_copy(part.at[0, c], fin.at[0], out_sem.at[2])
    stage_a(0)
    load_up.wait()
    load_down.wait()

    @pl.loop(0, pairs)
    def _(t):
        @pl.when(t > 0)
        def _():
            stage_a(2 * t)
            stage_c(t - 1)

        @pl.when(t >= 2)
        def _():
            stage_o(t - 2)

        @pl.when(t > 0)
        def _():
            stage_b(2 * t - 2)
            stage_b(2 * t - 1)

        stage_a(2 * t + 1)

    pl.loop(0, chips - 2)(stage_e)
    stage_c(pairs - 1)
    stage_b(chips - 2)
    stage_b(chips - 1)
    stage_o(pairs - 2)
    stage_e(chips - 2)
    stage_e(chips - 1)
    stage_o(pairs - 1)

    tile = min(256, dblk)

    @pl.loop(0, dblk // tile)
    def _(m):
        at = pl.ds(pl.multiple_of(k * dblk + m * tile, tile), tile)
        to = pl.ds(pl.multiple_of(m * tile, tile), tile)
        up_buf[to, :] = dot(xc[:, at], dhc[...], 0, 0).astype(BF16)

    put_up = pltpu.make_async_copy(up_buf, upg_hbm, out_sem.at[0])
    put_up.start()
    dtile = min(256, hq)

    @pl.loop(0, hq // dtile)
    def _(m):
        at = pl.ds(pl.multiple_of(m * dtile, dtile), dtile)
        down_buf[at, :] = dot(actc[:, at], dc[...], 0, 0).astype(BF16)

    put_down = pltpu.make_async_copy(down_buf, downg_hbm, out_sem.at[1])
    put_down.start()

    @pl.loop(1, chips)
    def _(i):
        home(i).wait_recv()

    @pl.loop(0, chips)
    def _(i):
        @pl.when(i > 0)
        def _():
            ici(i).wait_send()
            home(i).wait_send()

        half_sum(i).wait_send()
        for kk in range(dps):
            side(i, c, kk).wait_send()
        for j in range(1, dps):
            cross(i, other(j), k).wait_send()

    put_up.wait()
    put_down.wait()
    put_own.wait()


def one_hot(ids_ref, slots_ref, g, chips, rows):
    place = ids_ref[...] * rows + slots_ref[...]
    row = lax.broadcasted_iota(jnp.int32, (rows, place.shape[1]), 0)
    blocks = [jnp.where(place - xor(g, p, chips) * rows == row, 1.0, 0.0) for p in range(chips)]
    return jnp.concatenate(blocks, axis=0)


def finish(
    chips, cap, rows, ids_ref, slots_ref, gates_ref, fin, up_in, down_in,
    in_hbm, gate_ref, up_out, down_out, fin_buf, up_buf, down_buf, in_buf, sems,
):
    g = lax.axis_index("expert") // 2
    loads = [
        pltpu.make_async_copy(src, buf, sems.at[0, n])
        for n, (src, buf) in enumerate(((fin, fin_buf), (up_in, up_buf), (down_in, down_buf)))
    ]
    stores = [
        pltpu.make_async_copy(buf, dst, sems.at[1, n])
        for n, (buf, dst) in enumerate(((in_buf, in_hbm), (up_buf, up_out), (down_buf, down_out)))
    ]
    for load in loads:
        load.start()
    hot = one_hot(ids_ref, slots_ref, g, chips, rows)
    hot16 = hot.astype(BF16)
    for n in (1, 2):
        loads[n].wait()
        stores[n].start()
    loads[0].wait()
    half = fin_buf.shape[2]
    back = fin_buf[...].astype(F32)
    left = back[:, :rows].reshape(chips * rows, half).astype(BF16)
    right = back[:, rows:].reshape(chips * rows, half).astype(BF16)
    in_buf[:, :half] = dot(hot16, left, 0, 0).astype(BF16)
    in_buf[:, half:] = dot(hot16, right, 0, 0).astype(BF16)
    stores[0].start()
    eye = lax.broadcasted_iota(jnp.int32, (1, rows, 128), 1) == lax.broadcasted_iota(
        jnp.int32, (1, rows, 128), 2
    )
    col = jnp.sum(
        jnp.where(eye, back[:, cap : cap + 1, :128], 0.0), axis=2, keepdims=True
    ).reshape(chips * rows, 1)
    scaled = jnp.sum(hot * col, axis=0, keepdims=True)
    gates = gates_ref[...].astype(F32).reshape(1, -1)
    gate_ref[...] = (scaled / gates).astype(BF16).reshape(gate_ref.shape)
    for store in stores:
        store.wait()


def on_device(tokens_in, out_grad, gates, expert_ids, slot_ids, w_up, w_down):
    chips = lax.axis_size("expert") // 2
    dps = lax.axis_size("dp")
    tokens, width = tokens_in.shape
    hidden = w_up.shape[2]
    cap = 9 * tokens // (8 * chips)
    assert 1 <= cap % 8 <= 4
    rows = cap // 8 * 8 + 8
    hq = hidden // dps
    dblk = width // dps
    slots = 2 * dps * chips * rows
    vmem = pl.BlockSpec(memory_space=pltpu.VMEM)
    hbm = pl.BlockSpec(memory_space=pl.ANY)
    dma = pltpu.SemaphoreType.DMA
    ids = expert_ids.reshape(1, tokens)
    slot = slot_ids.reshape(1, tokens)
    raw = pl.pallas_call(
        functools.partial(kernel, chips, dps, cap, rows),
        out_shape=(
            jax.ShapeDtypeStruct((chips, 2 * rows, width // 2), BF16),
            jax.ShapeDtypeStruct((dblk, hidden), BF16),
            jax.ShapeDtypeStruct((hq, width), BF16),
        ),
        in_specs=[vmem] * 3 + [hbm] * 4,
        out_specs=(hbm,) * 3,
        scratch_shapes=[
            pltpu.VMEM((tokens, width), BF16),
            pltpu.VMEM((tokens, width), BF16),
            pltpu.VMEM((dblk, hidden), BF16),
            pltpu.VMEM((hq, width), BF16),
            pltpu.VMEM((chips, 2 * rows - 8, width), BF16),
            pltpu.VMEM((dps, chips, 2, 2 * rows - 8, width), BF16),
            pltpu.VMEM((slots, width), BF16),
            pltpu.VMEM((slots, width), BF16),
            pltpu.VMEM((slots, hq), BF16),
            pltpu.VMEM((slots, hidden), BF16),
            pltpu.VMEM((4 * rows, hidden), BF16),
            pltpu.VMEM((chips, 2, 2 * rows, width // 2), BF16),
            pltpu.VMEM((chips, 2 * rows, width // 2), BF16),
            pltpu.VMEM((width, hidden), BF16),
            pltpu.VMEM((hidden, width), BF16),
            dma((4,)),
            dma((3,)),
            dma((chips,)),
            dma((chips,)),
            dma((chips, dps)),
            dma((chips, dps)),
            dma((chips, dps)),
            dma((chips, dps)),
            dma((chips,)),
            dma((chips,)),
            dma((chips,)),
            dma((chips,)),
        ],
        compiler_params=pltpu.CompilerParams(
            collective_id=0, has_side_effects=True, vmem_limit_bytes=61 * 1024 * 1024
        ),
    )(ids, slot, gates, tokens_in, out_grad, w_up, w_down)
    in_grad, gate_grad, up_grad, down_grad = pl.pallas_call(
        functools.partial(finish, chips, cap, rows),
        out_shape=(
            jax.ShapeDtypeStruct((tokens, width), BF16),
            jax.ShapeDtypeStruct((tokens,), BF16),
            jax.ShapeDtypeStruct((dblk, hidden), BF16),
            jax.ShapeDtypeStruct((hq, width), BF16),
        ),
        in_specs=[vmem] * 3 + [hbm] * 3,
        out_specs=(hbm, vmem, hbm, hbm),
        scratch_shapes=[pltpu.VMEM(r.shape, r.dtype) for r in raw]
        + [pltpu.VMEM((tokens, width), BF16), dma((2, 3))],
        compiler_params=pltpu.CompilerParams(vmem_limit_bytes=32 * 1024 * 1024),
    )(ids, slot, gates, *raw)
    return (in_grad, gate_grad, up_grad[None], down_grad[None])


def solution(mesh):
    return jax.shard_map(
        on_device,
        mesh=mesh,
        in_specs=(
            P(("expert", "dp"), None),
            P(("expert", "dp"), None),
            P(("expert", "dp")),
            P(("expert", "dp")),
            P(("expert", "dp")),
            P("expert", None, None),
            P("expert", None, None),
        ),
        out_specs=(
            P(("expert", "dp"), None),
            P(("expert", "dp")),
            P("expert", "dp", None),
            P("expert", "dp", None),
        ),
        check_vma=False,
    )
```

```python
import functools

import jax
import jax.numpy as jnp
from jax import lax
from jax.experimental import pallas as pl
from jax.experimental.pallas import tpu as pltpu
from jax.sharding import PartitionSpec as P

F32 = jnp.float32
BF16 = jnp.bfloat16


def xor(a, b, count):
    total, bit = 0, 1
    while bit < count:
        total = total + lax.rem(a // bit + b // bit, 2) * bit
        bit *= 2
    return total


def gelu_parts(hidden):
    cdf = 0.5 * (1.0 + lax.erf(hidden * 0.7071067811865476))
    pdf = jnp.exp(-0.5 * hidden * hidden) * 0.3989422804014327
    return (hidden * cdf, cdf + hidden * pdf)


def dot(a, b, da, db):
    return lax.dot_general(a, b, (((da,), (db,)), ((), ())), preferred_element_type=F32)


def kernel(
    chips, dps, cap, rows,
    ids_ref, slots_ref, gates_ref, tok_hbm, cot_hbm, up_hbm, down_hbm,
    fin, upg_hbm, downg_hbm,
    tok_ref, cot_ref, up_buf, down_buf, tx, rx, xc, dc, actc, dhc, act_tmp,
    part, sib, wu, wd,
    w_sem, out_sem, ici_s, ici_r, sf_s, sf_r, xf_s, xf_r, ps_s, ps_r, fin_s, fin_r,
):
    me = lax.axis_index("expert")
    k = lax.axis_index("dp")
    g = me // 2
    c = lax.rem(me, 2)
    o = 1 - c
    tokens, width = tok_ref.shape
    half = width // 2
    hidden_dev = wu.shape[1]
    hq = hidden_dev // dps
    dblk = width // dps
    full = rows - 8
    pairs = chips // 2
    own_per = 4 * rows
    other_per = own_per * (dps - 1)
    mine = pl.ds(pl.multiple_of(k * hq, hq), hq)

    def dev(chip, core, dp):
        return {"expert": chip * 2 + core, "dp": dp}

    def other(j):
        return lax.rem(k + j, dps)

    def remote(src, dst, s, r, target):
        return pltpu.make_async_remote_copy(
            src_ref=src, dst_ref=dst, send_sem=s, recv_sem=r,
            device_id=target, device_id_type=pl.DeviceIdType.MESH,
        )

    def partner(p):
        return xor(g, p, chips)

    def ici(i):
        return remote(tx.at[i], rx.at[k, i, c], ici_s.at[i], ici_r.at[i], dev(partner(i), c, k))

    def side(i, core, kk):
        return remote(
            rx.at[kk, i, core], rx.at[kk, i, core], sf_s.at[i, kk], sf_r.at[i, kk], dev(g, o, k)
        )

    def cross(i, kk, slot):
        return remote(
            rx.at[slot, i, c], rx.at[slot, i, c], xf_s.at[i, kk], xf_r.at[i, slot], dev(g, c, kk)
        )

    def half_sum(i):
        return remote(part.at[i, o], sib.at[i], ps_s.at[i], ps_r.at[i], dev(g, o, k))

    def home(i):
        return remote(part.at[i, c], fin.at[i], fin_s.at[i], fin_r.at[i], dev(partner(i), c, k))

    load_tok = pltpu.make_async_copy(tok_hbm, tok_ref, w_sem.at[2])
    load_cot = pltpu.make_async_copy(cot_hbm, cot_ref, w_sem.at[3])
    load_up = pltpu.make_async_copy(up_hbm.at[0], wu, w_sem.at[0])
    load_down = pltpu.make_async_copy(down_hbm.at[0], wd, w_sem.at[1])
    load_tok.start()
    load_cot.start()

    barrier = pltpu.get_barrier_semaphore()

    def greet(target):
        pl.semaphore_signal(barrier, inc=1, device_id=target, device_id_type=pl.DeviceIdType.MESH)

    @pl.loop(1, chips)
    def _(i):
        greet(dev(partner(i), c, k))

    greet(dev(g, o, k))
    for j in range(1, dps):
        greet(dev(g, c, other(j)))

    eye = lax.broadcasted_iota(jnp.int32, (1, rows, 128), 1) == lax.broadcasted_iota(
        jnp.int32, (1, rows, 128), 2
    )
    at_cap = lax.broadcasted_iota(jnp.int32, (1, rows, 128), 1) == cap
    upper = lax.broadcasted_iota(jnp.int32, (1, 8, 1), 1) < 4

    def rolled(tiles8, shift):
        count = tiles8.shape[0]
        flat = pltpu.roll(tiles8.reshape(count * 8, width), shift, 0)
        return flat.reshape(count, 8, width)

    def pack(first, hot):
        count = hot.shape[0] // rows
        hot16 = hot.astype(BF16)
        gate_col = jnp.sum(hot * gates, axis=1, keepdims=True)
        x = dot(hot16, tok_ref[...], 1, 0).reshape(count, rows, width)
        d = (dot(hot16, cot_ref[...], 1, 0) * gate_col).reshape(count, rows, width)
        mixed = jnp.where(upper, x[:, full:], rolled(d[:, full:], 4))
        both = jnp.concatenate([x[:, :full], mixed, d[:, :full]], axis=1).astype(BF16)
        tx[first : first + count] = both
        if first == 0:
            rx[k, 0, c] = both[0]

    gates = gates_ref[...].astype(F32).reshape(1, -1)
    near = one_hot(ids_ref, slots_ref, g, chips, rows, range(chips // 2))
    far = one_hot(ids_ref, slots_ref, g, chips, rows, range(chips // 2, chips))
    load_tok.wait()
    load_cot.wait()
    load_up.start()
    load_down.start()
    pack(chips // 2, far)
    pl.semaphore_wait(barrier, chips - 1 + 1 + dps - 1)

    @pl.loop(chips // 2, chips)
    def _(i):
        ici(i).start()

    pack(0, near)

    @pl.loop(1, chips // 2)
    def _(i):
        ici(i).start()

    def stage_a(i):
        @pl.when(i > 0)
        def _():
            ici(i).wait_recv()

        for j in range(1, dps):
            cross(i, other(j), k).start()
        side(i, c, k).start()

    def stage_b(i):
        for j in range(1, dps):
            cross(i, other(j), other(j)).wait_recv()
            side(i, c, other(j)).start()

    def unpack(blk):
        blk = blk.astype(F32)
        count = blk.shape[0]
        mid = blk[:, full : full + 8]
        x_last = jnp.where(upper, mid, 0.0)
        d_last = jnp.where(upper, rolled(mid, count * 8 - 4), 0.0)
        x = jnp.concatenate([blk[:, :full], x_last], axis=1)
        d = jnp.concatenate([blk[:, full + 8 :], d_last], axis=1)
        return (
            x.reshape(count * rows, width).astype(BF16),
            d.reshape(count * rows, width).astype(BF16),
        )

    def stage_c(t):
        side(2 * t, o, k).wait_recv()
        side(2 * t + 1, o, k).wait_recv()
        x, d = unpack(rx[k, pl.ds(2 * t, 2)].reshape(4, 2 * full + 8, width))
        at = pl.ds(pl.multiple_of(t * own_per, own_per), own_per)
        xc[at, :] = x
        dc[at, :] = d
        value, slope = gelu_parts(dot(x, wu[...], 1, 0))
        d_act = dot(d, wd[...], 1, 1)
        act = value.astype(BF16)
        dh = (d_act * slope).astype(BF16)
        act_tmp[...] = act
        actc[at, :] = act_tmp[:, mine]
        dhc[at, :] = dh
        gp = jnp.sum(act.astype(F32) * d_act, axis=1, keepdims=True).reshape(4, rows, 1)
        gp_row = jnp.sum(jnp.where(eye, gp, 0.0), axis=1, keepdims=True)
        d_in = dot(dh, wu[...], 1, 1).reshape(4, rows, width)
        lead = jnp.where(at_cap, gp_row, d_in[:, :, :128])
        left = jnp.concatenate([lead, d_in[:, :, 128:half]], axis=2)
        whole = jnp.concatenate([left, d_in[:, :, half:]], axis=1).astype(BF16)
        part[pl.ds(2 * t, 2)] = whole.reshape(2, 2, 2 * rows, half)
        half_sum(2 * t).start()
        half_sum(2 * t + 1).start()

    def stage_o(t):
        for j in range(1, dps):
            kk = other(j)
            side(2 * t, o, kk).wait_recv()
            side(2 * t + 1, o, kk).wait_recv()
            x, d = unpack(rx[kk, pl.ds(2 * t, 2)].reshape(4, 2 * full + 8, width))
            at = pl.ds(
                pl.multiple_of(pairs * own_per + t * other_per + (j - 1) * own_per, own_per), own_per
            )
            xc[at, :] = x
            dc[at, :] = d
            value, slope = gelu_parts(dot(x, wu[...], 1, 0))
            d_act = dot(d, wd[...], 1, 1)
            act_tmp[...] = value.astype(BF16)
            actc[at, :] = act_tmp[:, mine]
            dhc[at, :] = (d_act * slope).astype(BF16)

    def stage_e(i):
        half_sum(i).wait_recv()
        total = (part[i, c].astype(F32) + sib[i].astype(F32)).astype(BF16)

        @pl.when(i > 0)
        def _():
            part[i, c] = total
            home(i).start()

        @pl.when(i == 0)
        def _():
            part[i, c] = total
            put_own.start()

    put_own = pltpu.make_async_copy(part.at[0, c], fin.at[0], out_sem.at[2])
    stage_a(0)
    load_up.wait()
    load_down.wait()

    @pl.loop(0, pairs)
    def _(t):
        @pl.when(t > 0)
        def _():
            stage_a(2 * t)
            stage_c(t - 1)

        @pl.when(t >= 2)
        def _():
            stage_o(t - 2)

        @pl.when(t > 0)
        def _():
            stage_b(2 * t - 2)
            stage_b(2 * t - 1)

        stage_a(2 * t + 1)

    pl.loop(0, chips - 2)(stage_e)
    stage_c(pairs - 1)
    stage_b(chips - 2)
    stage_b(chips - 1)
    stage_o(pairs - 2)
    stage_e(chips - 2)
    stage_e(chips - 1)
    stage_o(pairs - 1)

    tile = min(256, dblk)

    @pl.loop(0, dblk // tile)
    def _(m):
        at = pl.ds(pl.multiple_of(k * dblk + m * tile, tile), tile)
        to = pl.ds(pl.multiple_of(m * tile, tile), tile)
        up_buf[to, :] = dot(xc[:, at], dhc[...], 0, 0).astype(BF16)

    put_up = pltpu.make_async_copy(up_buf, upg_hbm, out_sem.at[0])
    put_up.start()
    dtile = min(256, hq)

    @pl.loop(0, hq // dtile)
    def _(m):
        at = pl.ds(pl.multiple_of(m * dtile, dtile), dtile)
        down_buf[at, :] = dot(actc[:, at], dc[...], 0, 0).astype(BF16)

    put_down = pltpu.make_async_copy(down_buf, downg_hbm, out_sem.at[1])
    put_down.start()

    @pl.loop(1, chips)
    def _(i):
        home(i).wait_recv()

    @pl.loop(0, chips)
    def _(i):
        @pl.when(i > 0)
        def _():
            ici(i).wait_send()
            home(i).wait_send()

        half_sum(i).wait_send()
        for kk in range(dps):
            side(i, c, kk).wait_send()
        for j in range(1, dps):
            cross(i, other(j), k).wait_send()

    put_up.wait()
    put_down.wait()
    put_own.wait()


def one_hot(ids_ref, slots_ref, g, chips, rows, positions):
    place = ids_ref[...] * rows + slots_ref[...]
    row = lax.broadcasted_iota(jnp.int32, (rows, place.shape[1]), 0)
    blocks = [jnp.where(place - xor(g, p, chips) * rows == row, 1.0, 0.0) for p in positions]
    return jnp.concatenate(blocks, axis=0)


def finish(
    chips, cap, rows, ids_ref, slots_ref, gates_ref, fin, up_in, down_in,
    in_hbm, gate_ref, up_out, down_out, fin_buf, up_buf, down_buf, in_buf, sems,
):
    g = lax.axis_index("expert") // 2
    loads = [
        pltpu.make_async_copy(src, buf, sems.at[0, n])
        for n, (src, buf) in enumerate(((fin, fin_buf), (up_in, up_buf), (down_in, down_buf)))
    ]
    stores = [
        pltpu.make_async_copy(buf, dst, sems.at[1, n])
        for n, (buf, dst) in enumerate(((in_buf, in_hbm), (up_buf, up_out), (down_buf, down_out)))
    ]
    for load in loads:
        load.start()
    hot = one_hot(ids_ref, slots_ref, g, chips, rows, range(chips))
    hot16 = hot.astype(BF16)
    for n in (1, 2):
        loads[n].wait()
        stores[n].start()
    loads[0].wait()
    half = fin_buf.shape[2]
    back = fin_buf[...].astype(F32)
    left = back[:, :rows].reshape(chips * rows, half).astype(BF16)
    right = back[:, rows:].reshape(chips * rows, half).astype(BF16)
    in_buf[:, :half] = dot(hot16, left, 0, 0).astype(BF16)
    in_buf[:, half:] = dot(hot16, right, 0, 0).astype(BF16)
    stores[0].start()
    eye = lax.broadcasted_iota(jnp.int32, (1, rows, 128), 1) == lax.broadcasted_iota(
        jnp.int32, (1, rows, 128), 2
    )
    col = jnp.sum(
        jnp.where(eye, back[:, cap : cap + 1, :128], 0.0), axis=2, keepdims=True
    ).reshape(chips * rows, 1)
    scaled = jnp.sum(hot * col, axis=0, keepdims=True)
    gates = gates_ref[...].astype(F32).reshape(1, -1)
    gate_ref[...] = (scaled / gates).astype(BF16).reshape(gate_ref.shape)
    for store in stores:
        store.wait()


def on_device(tokens_in, out_grad, gates, expert_ids, slot_ids, w_up, w_down):
    chips = lax.axis_size("expert") // 2
    dps = lax.axis_size("dp")
    tokens, width = tokens_in.shape
    hidden = w_up.shape[2]
    cap = 9 * tokens // (8 * chips)
    assert 1 <= cap % 8 <= 4
    rows = cap // 8 * 8 + 8
    hq = hidden // dps
    dblk = width // dps
    slots = 2 * dps * chips * rows
    vmem = pl.BlockSpec(memory_space=pltpu.VMEM)
    hbm = pl.BlockSpec(memory_space=pl.ANY)
    dma = pltpu.SemaphoreType.DMA
    ids = expert_ids.reshape(1, tokens)
    slot = slot_ids.reshape(1, tokens)
    raw = pl.pallas_call(
        functools.partial(kernel, chips, dps, cap, rows),
        out_shape=(
            jax.ShapeDtypeStruct((chips, 2 * rows, width // 2), BF16),
            jax.ShapeDtypeStruct((dblk, hidden), BF16),
            jax.ShapeDtypeStruct((hq, width), BF16),
        ),
        in_specs=[vmem] * 3 + [hbm] * 4,
        out_specs=(hbm,) * 3,
        scratch_shapes=[
            pltpu.VMEM((tokens, width), BF16),
            pltpu.VMEM((tokens, width), BF16),
            pltpu.VMEM((dblk, hidden), BF16),
            pltpu.VMEM((hq, width), BF16),
            pltpu.VMEM((chips, 2 * rows - 8, width), BF16),
            pltpu.VMEM((dps, chips, 2, 2 * rows - 8, width), BF16),
            pltpu.VMEM((slots, width), BF16),
            pltpu.VMEM((slots, width), BF16),
            pltpu.VMEM((slots, hq), BF16),
            pltpu.VMEM((slots, hidden), BF16),
            pltpu.VMEM((4 * rows, hidden), BF16),
            pltpu.VMEM((chips, 2, 2 * rows, width // 2), BF16),
            pltpu.VMEM((chips, 2 * rows, width // 2), BF16),
            pltpu.VMEM((width, hidden), BF16),
            pltpu.VMEM((hidden, width), BF16),
            dma((4,)),
            dma((3,)),
            dma((chips,)),
            dma((chips,)),
            dma((chips, dps)),
            dma((chips, dps)),
            dma((chips, dps)),
            dma((chips, dps)),
            dma((chips,)),
            dma((chips,)),
            dma((chips,)),
            dma((chips,)),
        ],
        compiler_params=pltpu.CompilerParams(
            collective_id=0, has_side_effects=True, vmem_limit_bytes=61 * 1024 * 1024
        ),
    )(ids, slot, gates, tokens_in, out_grad, w_up, w_down)
    in_grad, gate_grad, up_grad, down_grad = pl.pallas_call(
        functools.partial(finish, chips, cap, rows),
        out_shape=(
            jax.ShapeDtypeStruct((tokens, width), BF16),
            jax.ShapeDtypeStruct((tokens,), BF16),
            jax.ShapeDtypeStruct((dblk, hidden), BF16),
            jax.ShapeDtypeStruct((hq, width), BF16),
        ),
        in_specs=[vmem] * 3 + [hbm] * 3,
        out_specs=(hbm, vmem, hbm, hbm),
        scratch_shapes=[pltpu.VMEM(r.shape, r.dtype) for r in raw]
        + [pltpu.VMEM((tokens, width), BF16), dma((2, 3))],
        compiler_params=pltpu.CompilerParams(vmem_limit_bytes=61 * 1024 * 1024),
    )(ids, slot, gates, *raw)
    return (in_grad, gate_grad, up_grad[None], down_grad[None])


def solution(mesh):
    return jax.shard_map(
        on_device,
        mesh=mesh,
        in_specs=(
            P(("expert", "dp"), None),
            P(("expert", "dp"), None),
            P(("expert", "dp")),
            P(("expert", "dp")),
            P(("expert", "dp")),
            P("expert", None, None),
            P("expert", None, None),
        ),
        out_specs=(
            P(("expert", "dp"), None),
            P(("expert", "dp")),
            P("expert", "dp", None),
            P("expert", "dp", None),
        ),
        check_vma=False,
    )
```

```python
import functools

import jax
import jax.numpy as jnp
from jax import lax
from jax.experimental import pallas as pl
from jax.experimental.pallas import tpu as pltpu
from jax.sharding import PartitionSpec as P

F32 = jnp.float32
BF16 = jnp.bfloat16


def xor(a, b, count):
    total, bit = 0, 1
    while bit < count:
        total = total + lax.rem(a // bit + b // bit, 2) * bit
        bit *= 2
    return total


def gelu_parts(hidden):
    cdf = 0.5 * (1.0 + lax.erf(hidden * 0.7071067811865476))
    pdf = jnp.exp(-0.5 * hidden * hidden) * 0.3989422804014327
    return (hidden * cdf, cdf + hidden * pdf)


def dot(a, b, da, db):
    return lax.dot_general(a, b, (((da,), (db,)), ((), ())), preferred_element_type=F32)


def kernel(
    chips, dps, cap, rows,
    ids_ref, slots_ref, gates_ref, tok_hbm, cot_hbm, up_hbm, down_hbm,
    fin, upg_hbm, downg_hbm,
    tok_ref, cot_ref, up_buf, down_buf, tx, rx, xc, dc, actc, dhc, act_tmp,
    part, sib, wu, wd,
    w_sem, out_sem, ici_s, ici_r, sf_s, sf_r, xf_s, xf_r, ps_s, ps_r, fin_s, fin_r,
):
    me = lax.axis_index("expert")
    k = lax.axis_index("dp")
    g = me // 2
    c = lax.rem(me, 2)
    o = 1 - c
    tokens, width = tok_ref.shape
    half = width // 2
    hidden_dev = wu.shape[1]
    hq = hidden_dev // dps
    dblk = width // dps
    full = rows - 8
    pairs = chips // 2
    own_per = 4 * rows
    other_per = own_per * (dps - 1)
    mine = pl.ds(pl.multiple_of(k * hq, hq), hq)

    def dev(chip, core, dp):
        return {"expert": chip * 2 + core, "dp": dp}

    def other(j):
        return lax.rem(k + j, dps)

    def remote(src, dst, s, r, target):
        return pltpu.make_async_remote_copy(
            src_ref=src, dst_ref=dst, send_sem=s, recv_sem=r,
            device_id=target, device_id_type=pl.DeviceIdType.MESH,
        )

    def partner(p):
        return xor(g, p, chips)

    def ici(i):
        return remote(tx.at[i], rx.at[k, i, c], ici_s.at[i], ici_r.at[i], dev(partner(i), c, k))

    def side(i, core, kk):
        return remote(
            rx.at[kk, i, core], rx.at[kk, i, core], sf_s.at[i, kk], sf_r.at[i, kk], dev(g, o, k)
        )

    def cross(i, kk, slot):
        return remote(
            rx.at[slot, i, c], rx.at[slot, i, c], xf_s.at[i, kk], xf_r.at[i, slot], dev(g, c, kk)
        )

    def half_sum(i):
        return remote(part.at[i, o], sib.at[i], ps_s.at[i], ps_r.at[i], dev(g, o, k))

    def home(i):
        return remote(part.at[i, c], fin.at[i], fin_s.at[i], fin_r.at[i], dev(partner(i), c, k))

    load_tok = pltpu.make_async_copy(tok_hbm, tok_ref, w_sem.at[2])
    load_cot = pltpu.make_async_copy(cot_hbm, cot_ref, w_sem.at[3])
    load_up = pltpu.make_async_copy(up_hbm.at[0], wu, w_sem.at[0])
    load_down = pltpu.make_async_copy(down_hbm.at[0], wd, w_sem.at[1])
    load_tok.start()
    load_cot.start()
    load_up.start()
    load_down.start()

    barrier = pltpu.get_barrier_semaphore()

    def greet(target):
        pl.semaphore_signal(barrier, inc=1, device_id=target, device_id_type=pl.DeviceIdType.MESH)

    @pl.loop(1, chips)
    def _(i):
        greet(dev(partner(i), c, k))

    greet(dev(g, o, k))
    for j in range(1, dps):
        greet(dev(g, c, other(j)))

    eye = lax.broadcasted_iota(jnp.int32, (1, rows, 128), 1) == lax.broadcasted_iota(
        jnp.int32, (1, rows, 128), 2
    )
    at_cap = lax.broadcasted_iota(jnp.int32, (1, rows, 128), 1) == cap
    upper = lax.broadcasted_iota(jnp.int32, (1, 8, 1), 1) < 4

    def rolled(tiles8, shift):
        count = tiles8.shape[0]
        flat = pltpu.roll(tiles8.reshape(count * 8, width), shift, 0)
        return flat.reshape(count, 8, width)

    hot = one_hot(ids_ref, slots_ref, g, chips, rows)
    hot16 = hot.astype(BF16)
    gates = gates_ref[...].astype(F32).reshape(1, -1)
    gate_col = jnp.sum(hot * gates, axis=1, keepdims=True)
    load_tok.wait()
    load_cot.wait()
    x_pack = dot(hot16, tok_ref[...], 1, 0).reshape(chips, rows, width)
    d_pack = (dot(hot16, cot_ref[...], 1, 0) * gate_col).reshape(chips, rows, width)
    mixed = jnp.where(upper, x_pack[:, full:], rolled(d_pack[:, full:], 4))
    both = jnp.concatenate([x_pack[:, :full], mixed, d_pack[:, :full]], axis=1).astype(BF16)
    tx[...] = both
    rx[k, 0, c] = both[0]

    pl.semaphore_wait(barrier, chips - 1 + 1 + dps - 1)

    ici(chips // 2).start()

    @pl.loop(1, chips // 2)
    def _(i):
        ici(i).start()
        ici(chips // 2 + i).start()

    def stage_a(i):
        @pl.when(i > 0)
        def _():
            ici(i).wait_recv()

        for j in range(1, dps):
            cross(i, other(j), k).start()
        side(i, c, k).start()

    def stage_b(i):
        for j in range(1, dps):
            cross(i, other(j), other(j)).wait_recv()
            side(i, c, other(j)).start()

    def unpack(blk):
        blk = blk.astype(F32)
        count = blk.shape[0]
        mid = blk[:, full : full + 8]
        x_last = jnp.where(upper, mid, 0.0)
        d_last = jnp.where(upper, rolled(mid, count * 8 - 4), 0.0)
        x = jnp.concatenate([blk[:, :full], x_last], axis=1)
        d = jnp.concatenate([blk[:, full + 8 :], d_last], axis=1)
        return (
            x.reshape(count * rows, width).astype(BF16),
            d.reshape(count * rows, width).astype(BF16),
        )

    def stage_c(t):
        side(2 * t, o, k).wait_recv()
        side(2 * t + 1, o, k).wait_recv()
        x, d = unpack(rx[k, pl.ds(2 * t, 2)].reshape(4, 2 * full + 8, width))
        at = pl.ds(pl.multiple_of(t * own_per, own_per), own_per)
        xc[at, :] = x
        dc[at, :] = d
        value, slope = gelu_parts(dot(x, wu[...], 1, 0))
        d_act = dot(d, wd[...], 1, 1)
        act = value.astype(BF16)
        dh = (d_act * slope).astype(BF16)
        act_tmp[...] = act
        actc[at, :] = act_tmp[:, mine]
        dhc[at, :] = dh
        gp = jnp.sum(act.astype(F32) * d_act, axis=1, keepdims=True).reshape(4, rows, 1)
        gp_row = jnp.sum(jnp.where(eye, gp, 0.0), axis=1, keepdims=True)
        d_in = dot(dh, wu[...], 1, 1).reshape(4, rows, width)
        lead = jnp.where(at_cap, gp_row, d_in[:, :, :128])
        left = jnp.concatenate([lead, d_in[:, :, 128:half]], axis=2)
        whole = jnp.concatenate([left, d_in[:, :, half:]], axis=1).astype(BF16)
        part[pl.ds(2 * t, 2)] = whole.reshape(2, 2, 2 * rows, half)
        half_sum(2 * t).start()
        half_sum(2 * t + 1).start()

    def stage_o(t):
        for j in range(1, dps):
            kk = other(j)
            side(2 * t, o, kk).wait_recv()
            side(2 * t + 1, o, kk).wait_recv()
            x, d = unpack(rx[kk, pl.ds(2 * t, 2)].reshape(4, 2 * full + 8, width))
            at = pl.ds(
                pl.multiple_of(pairs * own_per + t * other_per + (j - 1) * own_per, own_per), own_per
            )
            xc[at, :] = x
            dc[at, :] = d
            value, slope = gelu_parts(dot(x, wu[...], 1, 0))
            d_act = dot(d, wd[...], 1, 1)
            act_tmp[...] = value.astype(BF16)
            actc[at, :] = act_tmp[:, mine]
            dhc[at, :] = (d_act * slope).astype(BF16)

    def stage_e(i):
        half_sum(i).wait_recv()
        total = (part[i, c].astype(F32) + sib[i].astype(F32)).astype(BF16)

        @pl.when(i > 0)
        def _():
            part[i, c] = total
            home(i).start()

        @pl.when(i == 0)
        def _():
            part[i, c] = total
            put_own.start()

    put_own = pltpu.make_async_copy(part.at[0, c], fin.at[0], out_sem.at[2])
    stage_a(0)
    load_up.wait()
    load_down.wait()

    @pl.loop(0, pairs)
    def _(t):
        @pl.when(t > 0)
        def _():
            stage_a(2 * t)
            stage_c(t - 1)

        @pl.when(t >= 2)
        def _():
            stage_o(t - 2)

        @pl.when(t > 0)
        def _():
            stage_b(2 * t - 2)
            stage_b(2 * t - 1)

        stage_a(2 * t + 1)

    pl.loop(0, chips - 2)(stage_e)
    stage_c(pairs - 1)
    stage_b(chips - 2)
    stage_b(chips - 1)
    stage_o(pairs - 2)
    stage_e(chips - 2)
    stage_e(chips - 1)
    stage_o(pairs - 1)

    tile = min(256, dblk)

    @pl.loop(0, dblk // tile)
    def _(m):
        at = pl.ds(pl.multiple_of(k * dblk + m * tile, tile), tile)
        to = pl.ds(pl.multiple_of(m * tile, tile), tile)
        up_buf[to, :] = dot(xc[:, at], dhc[...], 0, 0).astype(BF16)

    put_up = pltpu.make_async_copy(up_buf, upg_hbm, out_sem.at[0])
    put_up.start()
    dtile = min(256, hq)

    @pl.loop(0, hq // dtile)
    def _(m):
        at = pl.ds(pl.multiple_of(m * dtile, dtile), dtile)
        down_buf[at, :] = dot(actc[:, at], dc[...], 0, 0).astype(BF16)

    put_down = pltpu.make_async_copy(down_buf, downg_hbm, out_sem.at[1])
    put_down.start()

    @pl.loop(1, chips)
    def _(i):
        home(i).wait_recv()

    @pl.loop(0, chips)
    def _(i):
        @pl.when(i > 0)
        def _():
            ici(i).wait_send()
            home(i).wait_send()

        half_sum(i).wait_send()
        for kk in range(dps):
            side(i, c, kk).wait_send()
        for j in range(1, dps):
            cross(i, other(j), k).wait_send()

    put_up.wait()
    put_down.wait()
    put_own.wait()


def one_hot(ids_ref, slots_ref, g, chips, rows):
    place = ids_ref[...] * rows + slots_ref[...]
    row = lax.broadcasted_iota(jnp.int32, (rows, place.shape[1]), 0)
    blocks = [jnp.where(place - xor(g, p, chips) * rows == row, 1.0, 0.0) for p in range(chips)]
    return jnp.concatenate(blocks, axis=0)


def finish(
    chips, cap, rows, ids_ref, slots_ref, gates_ref, fin, up_in, down_in,
    in_hbm, gate_ref, up_out, down_out, fin_buf, up_buf, down_buf, in_buf, sems,
):
    g = lax.axis_index("expert") // 2
    loads = [
        pltpu.make_async_copy(src, buf, sems.at[0, n])
        for n, (src, buf) in enumerate(((fin, fin_buf), (up_in, up_buf), (down_in, down_buf)))
    ]
    stores = [
        pltpu.make_async_copy(buf, dst, sems.at[1, n])
        for n, (buf, dst) in enumerate(((in_buf, in_hbm), (up_buf, up_out), (down_buf, down_out)))
    ]
    for load in loads:
        load.start()
    hot = one_hot(ids_ref, slots_ref, g, chips, rows)
    hot16 = hot.astype(BF16)
    for n in (1, 2):
        loads[n].wait()
        stores[n].start()
    loads[0].wait()
    half = fin_buf.shape[2]
    back = fin_buf[...].astype(F32)
    left = back[:, :rows].reshape(chips * rows, half).astype(BF16)
    right = back[:, rows:].reshape(chips * rows, half).astype(BF16)
    in_buf[:, :half] = dot(hot16, left, 0, 0).astype(BF16)
    in_buf[:, half:] = dot(hot16, right, 0, 0).astype(BF16)
    stores[0].start()
    eye = lax.broadcasted_iota(jnp.int32, (1, rows, 128), 1) == lax.broadcasted_iota(
        jnp.int32, (1, rows, 128), 2
    )
    col = jnp.sum(
        jnp.where(eye, back[:, cap : cap + 1, :128], 0.0), axis=2, keepdims=True
    ).reshape(chips * rows, 1)
    scaled = jnp.sum(hot * col, axis=0, keepdims=True)
    gates = gates_ref[...].astype(F32).reshape(1, -1)
    gate_ref[...] = (scaled / gates).astype(BF16).reshape(gate_ref.shape)
    for store in stores:
        store.wait()


def on_device(tokens_in, out_grad, gates, expert_ids, slot_ids, w_up, w_down):
    chips = lax.axis_size("expert") // 2
    dps = lax.axis_size("dp")
    tokens, width = tokens_in.shape
    hidden = w_up.shape[2]
    cap = 9 * tokens // (8 * chips)
    assert 1 <= cap % 8 <= 4
    rows = cap // 8 * 8 + 8
    hq = hidden // dps
    dblk = width // dps
    slots = 2 * dps * chips * rows
    vmem = pl.BlockSpec(memory_space=pltpu.VMEM)
    hbm = pl.BlockSpec(memory_space=pl.ANY)
    dma = pltpu.SemaphoreType.DMA
    ids = expert_ids.reshape(1, tokens)
    slot = slot_ids.reshape(1, tokens)
    held = chips * 2 * rows * width * (1 + 2 * dps + 2 + 1) + slots * (2 * width + hq + hidden)
    held += 2 * hidden * width + tokens * 2 * width + dblk * hidden + hq * width + 4 * rows * hidden
    limit = (49 if 2 * held < 40 * 2**20 else 61) * 2**20
    raw = pl.pallas_call(
        functools.partial(kernel, chips, dps, cap, rows),
        out_shape=(
            jax.ShapeDtypeStruct((chips, 2 * rows, width // 2), BF16),
            jax.ShapeDtypeStruct((dblk, hidden), BF16),
            jax.ShapeDtypeStruct((hq, width), BF16),
        ),
        in_specs=[vmem] * 3 + [hbm] * 4,
        out_specs=(hbm,) * 3,
        scratch_shapes=[
            pltpu.VMEM((tokens, width), BF16),
            pltpu.VMEM((tokens, width), BF16),
            pltpu.VMEM((dblk, hidden), BF16),
            pltpu.VMEM((hq, width), BF16),
            pltpu.VMEM((chips, 2 * rows - 8, width), BF16),
            pltpu.VMEM((dps, chips, 2, 2 * rows - 8, width), BF16),
            pltpu.VMEM((slots, width), BF16),
            pltpu.VMEM((slots, width), BF16),
            pltpu.VMEM((slots, hq), BF16),
            pltpu.VMEM((slots, hidden), BF16),
            pltpu.VMEM((4 * rows, hidden), BF16),
            pltpu.VMEM((chips, 2, 2 * rows, width // 2), BF16),
            pltpu.VMEM((chips, 2 * rows, width // 2), BF16),
            pltpu.VMEM((width, hidden), BF16),
            pltpu.VMEM((hidden, width), BF16),
            dma((4,)),
            dma((3,)),
            dma((chips,)),
            dma((chips,)),
            dma((chips, dps)),
            dma((chips, dps)),
            dma((chips, dps)),
            dma((chips, dps)),
            dma((chips,)),
            dma((chips,)),
            dma((chips,)),
            dma((chips,)),
        ],
        compiler_params=pltpu.CompilerParams(
            collective_id=0, has_side_effects=True, vmem_limit_bytes=limit
        ),
    )(ids, slot, gates, tokens_in, out_grad, w_up, w_down)
    in_grad, gate_grad, up_grad, down_grad = pl.pallas_call(
        functools.partial(finish, chips, cap, rows),
        out_shape=(
            jax.ShapeDtypeStruct((tokens, width), BF16),
            jax.ShapeDtypeStruct((tokens,), BF16),
            jax.ShapeDtypeStruct((dblk, hidden), BF16),
            jax.ShapeDtypeStruct((hq, width), BF16),
        ),
        in_specs=[vmem] * 3 + [hbm] * 3,
        out_specs=(hbm, vmem, hbm, hbm),
        scratch_shapes=[pltpu.VMEM(r.shape, r.dtype) for r in raw]
        + [pltpu.VMEM((tokens, width), BF16), dma((2, 3))],
        compiler_params=pltpu.CompilerParams(vmem_limit_bytes=32 * 1024 * 1024),
    )(ids, slot, gates, *raw)
    return (in_grad, gate_grad, up_grad[None], down_grad[None])


def solution(mesh):
    return jax.shard_map(
        on_device,
        mesh=mesh,
        in_specs=(
            P(("expert", "dp"), None),
            P(("expert", "dp"), None),
            P(("expert", "dp")),
            P(("expert", "dp")),
            P(("expert", "dp")),
            P("expert", None, None),
            P("expert", None, None),
        ),
        out_specs=(
            P(("expert", "dp"), None),
            P(("expert", "dp")),
            P("expert", "dp", None),
            P("expert", "dp", None),
        ),
        check_vma=False,
    )
```
